512 devices in a mesh: row: 16 (over y, core), col: 32 (over z, x).
Axes of the slice: x: 4, y: 8, z: 8, core: 2. Of those that a mesh axis runs over, the one named last changes fastest.
Arguments:
- inside: float32 [2, 16, 1, 32, 256, 256], P(None, 'row', None, 'col'), may hold values from -0.375 to 0.375
- outer: float32 [2, 16, 1, 32, 256, 256], P(None, 'row', None, 'col'), may hold values from -6 to 6
- sequence: int32 [8192], replicated, may hold values from 0 to 3
Outputs:
- window: float32 [3, 2, 16, 256, 256], P(None, None, 'row', 'col')
The draws below stay inside these ranges and needn't reach their ends.
Inputs may be any that keep to these rules, and one draw needn't show every extreme that they name: `sequence`: codes 0 A, 1 C, 2 G, 3 U.
All inputs are finite; a program needn't handle non-finite values.
Results may differ from the reference program's by a relative error of at most 0.0001.
Values sent between devices are 32-bit elements; how exact they have to be, the bound alone decides.
No kernel may reach another device: no remote copies, remote signals or barrier semaphores. Data moves between devices by JAX's collectives and lax.ppermute only.
A program may use at most 64 MiB of HBM per device.

```python
import jax
import jax.numpy as jnp
from jax import lax

B = 256
CT = 1
TOP = 4
WIN = 3
RT = 2
LEN = 8192
N_ROW = 16
N_COL = 32


def with_ends(values, stream_key, low, high):
    index_at = [jax.random.randint(jax.random.fold_in(stream_key, axis), (), 0, length) for axis, length in enumerate(values.shape)]
    longest = values.shape.index(max(values.shape))
    neighbour = index_at[:longest] + [(index_at[longest] + 1) % values.shape[longest]] + index_at[longest + 1:]
    return values.at[tuple(index_at)].set(low).at[tuple(neighbour)].set(high)


def level_of(rng, extent, cuts, low, high):
    level, own = 1.0, jax.random.fold_in(rng, 6)
    for dim, shards_of in cuts:
        steps = jnp.exp(jax.random.uniform(jax.random.fold_in(own, dim), (shards_of,), jnp.float32, low / len(cuts), high / len(cuts)))
        level = level * jnp.repeat(steps, extent[dim] // shards_of).reshape([-1 if axis == dim else 1 for axis in range(len(extent))])
    return level


def noise(key, shape, scale, reach, split=(), held_as=jnp.bfloat16):
    result = jax.random.normal(key, shape, jnp.float32) * scale
    if len(split) > 0:
        result = level_of(key, shape, split, -0.22, 0.18) * result
    return jnp.clip(result, min=-reach, max=reach).astype(held_as)


def setup_inputs(seed: int = 0) -> dict:
    splits = jax.random.split(jax.random.key(seed), 4)
    inside = noise(splits[0], (RT, N_ROW, CT, N_COL, B, B), B ** -0.5, 0.375, ((1, 16), (3, 32)), jnp.float32)
    outer = noise(splits[1], (RT, N_ROW, CT, N_COL, B, B), 1.0, 6.0, ((1, 16), (3, 32)), jnp.float32)
    sequence = with_ends(jax.random.randint(splits[2], (LEN,), 0, 4), jax.random.fold_in(splits[2], 1), 0, 3).astype(jnp.int32)
    return {"inside": inside, "outer": outer, "sequence": sequence}


def pair_allowed(codes_left, codes_right, start_left, start_right):
    offsets = jnp.arange(B).astype(jnp.int32)
    total = codes_left[:, None] + codes_right[None, :]
    left_pos = start_left + offsets
    right_pos = start_right + offsets
    return ((total == 3) | (total == 5)) & ((right_pos[None, :] - left_pos[:, None]) > 3)


def reference(inside, outer, sequence):
    tile_count = CT * N_COL
    ins = inside.reshape(tile_count, tile_count, B, B)
    outs = outer.reshape(tile_count, tile_count, B, B)
    codes = sequence.reshape(tile_count, B)
    factor = 1.0 / (tile_count ** 0.5)
    computed = {}
    results = []
    for window_step in range(WIN):
        diagonal = TOP - window_step
        row_list = []
        for row_tile in range(tile_count):
            inner_row = row_tile + diagonal
            if inner_row >= tile_count:
                row_list.append(jnp.zeros((B, B), outs.dtype))
                continue
            accum = jnp.zeros((B, B), outs.dtype)
            for col_tile in range(inner_row + 1, tile_count):
                if col_tile - row_tile > TOP:
                    left_tile = outs[row_tile, col_tile]
                else:
                    left_tile = computed[(row_tile, col_tile)]
                allowed = pair_allowed(codes[inner_row], codes[col_tile], inner_row * B, col_tile * B)
                masked = jnp.where(allowed, ins[inner_row, col_tile], 0.0)
                accum = accum + jnp.dot(left_tile, masked.T, precision=lax.Precision.HIGHEST)
            new_tile = outs[row_tile, inner_row] + factor * accum
            computed[(row_tile, inner_row)] = new_tile
            row_list.append(new_tile)
        results.append(jnp.stack(row_list))
    return jnp.stack(results).reshape(WIN, tile_count // N_ROW, N_ROW, B, B)
```

```python
import math

import jax
import jax.numpy as jnp
import numpy as np
from jax import lax
from jax.sharding import Mesh, PartitionSpec as P

TOP = 4
WIN = 3
AXES = ("y", "core", "zh", "zl", "x")


def pairs_of(sizes, target):
    pairs = []
    for number in range(math.prod(sizes)):
        there = target(*np.unravel_index(number, sizes))
        pairs.append((number, int(np.ravel_multi_index(there, sizes))))
    return pairs


def on_device(sizes, inside, outer, sequence):
    rows_count = sizes[0] * sizes[1]
    cols_count = sizes[2] * sizes[3] * sizes[4]
    size = inside.shape[-1]
    slots = inside.shape[0]
    tile_count = slots * rows_count
    part = slots * size // cols_count
    factor = 1.0 / math.sqrt(tile_count)
    core = lax.axis_index("core")
    row = lax.axis_index("y") * sizes[1] + core
    half = lax.axis_index("zh")
    col = lax.axis_index(AXES[2:])
    home = inside[:, 0, 0, 0]
    out_tiles = outer[:, 0, 0, 0]

    def row_shift(x, by):
        n = sizes[0]
        return lax.ppermute(x, "y", [(i, (i + by) % n) for i in range(n)])

    left = row_shift(out_tiles, 1)
    ahead = row_shift(home, -1)
    left = jnp.where(row < 2, jnp.stack([jnp.zeros_like(left[0]), left[0]]), left)
    ahead = jnp.where(row >= rows_count - 2, jnp.stack([ahead[1], ahead[0]]), ahead)
    beside = lax.ppermute(jnp.where(core == 1, home, ahead), "core", [(0, 1), (1, 0)])

    slot = jnp.arange(slots, dtype=jnp.int32)
    tile_row = slot * rows_count + row - 2
    codes = sequence.reshape(tile_count, size)
    offsets = jnp.arange(size, dtype=jnp.int32)
    col_codes = lax.dynamic_index_in_dim(codes, col, 0, False)
    col_pos = col * size + offsets

    def masked(tiles, rows):
        row_codes = jnp.take(codes, jnp.clip(rows, 0, tile_count - 1), axis=0)
        total = row_codes[:, :, None] + col_codes[None, None, :]
        far = col_pos[None, None, :] - (rows[:, None] * size + offsets)[:, :, None] > 3
        return jnp.where(((total == 3) | (total == 5)) & far, tiles, 0.0)

    gap = col - row
    near = masked(home, slot * rows_count + row)
    mine = jnp.where((gap == 1) | (gap == 2), near[0], near[1])
    mine = mine.reshape(1, size // part, part, size)
    spread = jnp.broadcast_to(mine, (slots,) + mine.shape[1:]).reshape(cols_count, part, size)
    spread = lax.all_to_all(spread, AXES[2:], 0, 0)
    first = jnp.minimum(row + half * rows_count + 1, cols_count - 1)
    second = jnp.minimum(row + half * rows_count + 2, cols_count - 1)
    near1 = lax.dynamic_index_in_dim(spread, first, 0, False)
    near2 = lax.dynamic_index_in_dim(spread, second, 0, False)

    def previous_row(y, c, zh, zl, x):
        r = y * sizes[1] + c
        zh = zh if r > 0 else (zh + 1) % sizes[2]
        r = (r - 1) % rows_count
        return r // sizes[1], r % sizes[1], zh, zl, x

    next1 = lax.ppermute(near1, AXES, pairs_of(sizes, previous_row))
    bits = jnp.stack([near1, near2, next1])
    bits = lax.all_to_all(jnp.broadcast_to(bits, (sizes[3],) + bits.shape), "zl", 0, 0)
    bits = lax.all_to_all(jnp.broadcast_to(bits, (sizes[4],) + bits.shape), "x", 0, 0)
    whole = jnp.transpose(bits, (2, 1, 0, 3, 4)).reshape(3, size, size)

    def summed(tiles, e):
        right = masked(tiles, tile_row + e)
        product = jnp.einsum("auv,awv->auw", left, right, precision=lax.Precision.HIGH)
        real = (tile_row >= 0)[:, None, None]
        inner = (col > tile_row + TOP)[:, None, None]
        own = (col == tile_row + e)[:, None, None]
        part_sum = jnp.where(real & inner, factor * product, jnp.where(real & own, left, 0.0))
        got = lax.all_to_all(part_sum.reshape(cols_count, part, size), AXES[2:], 0, 0)
        return jnp.sum(got, axis=0)

    sum2 = summed(home, 2)
    sum4 = summed(ahead, 4)
    sum3 = summed(beside, 3)

    def times(a, b):
        return factor * jnp.einsum("ru,ku->rk", a, b, precision=lax.Precision.HIGH)

    w4 = sum4
    w3 = sum3 + times(w4, whole[2])
    w2 = sum2 + times(w4, whole[1]) + times(w3, whole[0])
    result = jnp.stack([w4, w3, w2])

    def sent_to(flip):
        def target(y, c, zh, zl, x):
            r = (y * sizes[1] + c - 2) % rows_count
            pick = zh if flip == 0 else 1 - zh
            n = 2 * (zl * sizes[4] + x) + pick
            zl2 = n // sizes[4] % sizes[3]
            return r // sizes[1], r % sizes[1], n // (sizes[3] * sizes[4]), zl2, n % sizes[4]
        return target

    piece = part // slots
    split = result.reshape(WIN, slots, piece, size)
    got = []
    for flip in range(2):
        which = half if flip == 0 else 1 - half
        mine = lax.dynamic_index_in_dim(split, which, 1, False)
        got.append(lax.ppermute(mine, AXES, pairs_of(sizes, sent_to(flip))))
    swap = (col % 2 == 1) ^ (row >= rows_count - 2)
    low = jnp.where(swap, got[1], got[0])
    high = jnp.where(swap, got[0], got[1])
    return jnp.stack([low, high], 1)[:, :, None]


def solution(mesh):
    sizes = (mesh.shape["row"] // 2, 2, 2, mesh.shape["col"] // 8, 4)
    fine = Mesh(mesh.devices.reshape(sizes), AXES)
    rows, cols = AXES[:2], AXES[2:]
    placed = (P(None, rows, None, cols, None, None), P(None, rows, None, cols, None, None), P())
    return jax.shard_map(
        lambda *args: on_device(sizes, *args),
        mesh=fine,
        in_specs=placed,
        out_specs=P(None, None, rows, cols, None),
        check_vma=False,
    )
```

```python
import functools
import math

import jax
import jax.numpy as jnp
import numpy as np
from jax import lax
from jax.experimental import pallas as pl
from jax.experimental.pallas import tpu as pltpu
from jax.sharding import Mesh, PartitionSpec as P

TOP = 4
WIN = 3
AXES = ("y", "core", "zh", "zl", "x")
F32 = jnp.float32


def pairs_of(sizes, target):
    pairs = []
    for number in range(math.prod(sizes)):
        there = target(*(int(i) for i in np.unravel_index(number, sizes)))
        if there is not None:
            pairs.append((number, int(np.ravel_multi_index(there, sizes))))
    return pairs


def halves(x):
    high = x.astype(jnp.bfloat16)
    return high, (x - high.astype(F32)).astype(jnp.bfloat16)


def times(a, b):
    dims = (((1,), (1,)), ((), ()))
    dot = functools.partial(lax.dot_general, dimension_numbers=dims, preferred_element_type=F32)
    return dot(a[0], b[0]) + (dot(a[0], b[1]) + dot(a[1], b[0]))


def product_kernel(steps, tile_count, factor, place, left_ref, *refs):
    pick_count = len(steps)
    right_refs, (row_codes, col_codes), rest = refs[:pick_count], refs[pick_count:pick_count + 2], refs[pick_count + 2:]
    outs, full = rest[:-1], rest[-1]
    row, col, x = place[0], place[1], place[4]
    slots, size = left_ref.shape[0], left_ref.shape[1]
    rows_count = tile_count // slots
    block = size // len(outs)
    gap = lax.broadcasted_iota(jnp.int32, (size, size), 1) - lax.broadcasted_iota(jnp.int32, (size, size), 0)
    for slot in range(slots):
        tile_row = slot * rows_count + row - 2
        left = left_ref[jnp.where(row < 2, 0, slot)]
        left_halves = halves(left)
        live = (tile_row >= 0) & (col > tile_row + TOP)
        scale = jnp.where(live, factor, 0.0).astype(F32)
        for number, (e, tile_of) in enumerate(steps):
            tile = tile_of(right_refs[number], slot, row)
            total = row_codes[number, slot] + col_codes[...]
            allowed = ((total == 3) | (total == 5)) & (gap + (col - tile_row - e) * size > 3)
            right = halves(jnp.where(allowed, tile, 0.0))
            own = jnp.where((tile_row >= 0) & (col == tile_row + e), 1.0, 0.0).astype(F32)
            full[...] = scale * times(left_halves, right) + own * left
            for j, out in enumerate(outs):
                out[number, slot] = full[pl.ds(pl.multiple_of((x ^ j) * block, block), block), :]


def add_kernel(counts, *refs):
    out = refs[-1]
    parts = [refs[:counts], refs[counts:2 * counts]]
    slots, rows = parts[0][0].shape[1:3]
    deep = out.shape[0] // slots
    piece = rows // deep
    for group, number, place in ((0, 1, 0), (1, 0, 1), (0, 0, 2)):
        for slot in range(slots):
            total = parts[group][0][number, slot]
            for ref in parts[group][1:]:
                total = total + ref[number, slot]
            for z in range(deep):
                out[slot * deep + z, place] = total[z * piece:(z + 1) * piece]


def finish_kernel(factor, place, got, whole, out_a, out_b, rows):
    half = place[2]
    sums = []
    for w in range(WIN):
        total = got[0, w]
        for k in range(1, got.shape[0]):
            total = total + got[k, w]
        sums.append(total)
    tiles = [halves(whole[k]) for k in range(3)]
    w4 = sums[0]
    w4_halves = halves(w4)
    w3 = sums[1] + factor * times(w4_halves, tiles[2])
    w2 = sums[2] + factor * (times(w4_halves, tiles[1]) + times(halves(w3), tiles[0]))
    piece = out_a.shape[1]
    for w, value in enumerate((w4, w3, w2)):
        rows[w] = value
        out_a[w] = rows[w, pl.ds(pl.multiple_of(half * piece, piece), piece), :]
        out_b[w] = rows[w, pl.ds(pl.multiple_of((1 - half) * piece, piece), piece), :]


def call(kernel, in_count, outs, scratch, flops, *args):
    spec = pl.BlockSpec(memory_space=pltpu.VMEM)
    moved = sum(math.prod(a.shape) * 4 for a in args) + sum(math.prod(s) * 4 for s in outs)
    return pl.pallas_call(
        kernel,
        out_shape=[jax.ShapeDtypeStruct(s, F32) for s in outs],
        in_specs=[pl.BlockSpec(memory_space=pltpu.SMEM)] * in_count + [spec] * (len(args) - in_count),
        out_specs=[spec] * len(outs),
        scratch_shapes=scratch,
        cost_estimate=pl.CostEstimate(flops=flops, bytes_accessed=moved, transcendentals=0),
        compiler_params=pltpu.CompilerParams(vmem_limit_bytes=24 * 1024 * 1024),
    )(*args)


def on_device(sizes, inside, outer, sequence):
    rows_count = sizes[0] * sizes[1]
    cols_count = sizes[2] * sizes[3] * sizes[4]
    size = inside.shape[-1]
    slots = inside.shape[0]
    tile_count = slots * rows_count
    part = slots * size // cols_count
    factor = 1.0 / math.sqrt(tile_count)
    core = lax.axis_index("core")
    row = lax.axis_index("y") * sizes[1] + core
    half = lax.axis_index("zh")
    col = lax.axis_index(AXES[2:])
    place = jnp.stack([row, col, half, core, lax.axis_index("x")]).astype(jnp.int32)
    home = inside[:, 0, 0, 0]
    out_tiles = outer[:, 0, 0, 0]

    def row_shift(v, by):
        n = sizes[0]
        return lax.ppermute(v, "y", [(i, (i + by) % n) for i in range(n)])

    left = row_shift(out_tiles, 1)
    ahead = row_shift(home, -1)
    beside0 = lax.ppermute(home, "core", [(1, 0)])
    beside1 = lax.ppermute(ahead, "core", [(0, 1)])

    slot = jnp.arange(slots, dtype=jnp.int32)
    codes = sequence.reshape(tile_count, size)
    offsets = jnp.arange(size, dtype=jnp.int32)
    col_codes = lax.dynamic_index_in_dim(codes, col, 0, True)
    col_pos = col * size + offsets
    wanted = slot[None, :] * rows_count + row + jnp.arange(WIN, dtype=jnp.int32)[:, None]
    row_codes = jnp.take(codes, jnp.clip(wanted, 0, tile_count - 1), axis=0)

    gap = col - row
    early = (gap == 1) | (gap == 2)
    near_row = jnp.where(early, row, rows_count + row)
    near_codes = jnp.where(early, row_codes[0, 0], row_codes[0, 1])
    total = near_codes[:, None] + col_codes
    far = col_pos[None, :] - (near_row * size + offsets)[:, None] > 3
    near = jnp.where(((total == 3) | (total == 5)) & far, jnp.where(early, home[0], home[1]), 0.0)
    near = near.reshape(1, size // part, part, size)
    spread = jnp.broadcast_to(near, (slots,) + near.shape[1:]).reshape(cols_count, part, size)
    spread = lax.all_to_all(spread, AXES[2:], 0, 0)
    first = jnp.minimum(row + half * rows_count + 1, cols_count - 1)
    second = jnp.minimum(row + half * rows_count + 2, cols_count - 1)
    near1 = lax.dynamic_index_in_dim(spread, first, 0, False)
    near2 = lax.dynamic_index_in_dim(spread, second, 0, False)

    def previous_row(y, c, zh, zl, x):
        r = y * sizes[1] + c
        zh = zh if r > 0 else (zh + 1) % sizes[2]
        r = (r - 1) % rows_count
        return r // sizes[1], r % sizes[1], zh, zl, x

    next1 = lax.ppermute(near1, AXES, pairs_of(sizes, previous_row))
    bits = jnp.stack([near1, near2, next1])
    bits = lax.all_to_all(jnp.broadcast_to(bits, (sizes[3],) + bits.shape), "zl", 0, 0)
    bits = lax.all_to_all(jnp.broadcast_to(bits, (sizes[4],) + bits.shape), "x", 0, 0)
    whole = jnp.transpose(bits, (2, 1, 0, 3, 4)).reshape(WIN, size, size)

    def own_tile(ref, s, r):
        return ref[s]

    def ahead_tile(ref, s, r):
        return ref[jnp.where(r >= rows_count - 2, slots - 1 - s, s)]

    def beside_tile(ref, s, r):
        return ref[jnp.where(r >= rows_count - 1, slots - 1 - s, s)]

    def summed_parts(steps, rights, chosen):
        blocks = [(len(steps), slots, size // sizes[4], size)] * sizes[4]
        return call(
            functools.partial(product_kernel, steps, tile_count, factor),
            1, blocks, [pltpu.VMEM((size, size), F32)], len(steps) * slots * 6 * size**3,
            place, left, *rights, row_codes[chosen][..., None], col_codes,
        )

    def exchanged(parts):
        n = sizes[4]
        return [parts[0]] + [lax.ppermute(parts[j], "x", [(i, i ^ j) for i in range(n)]) for j in range(1, n)]

    parts24 = summed_parts([(2, own_tile), (4, ahead_tile)], [home, ahead], np.array([0, 2]))
    parts24 = exchanged(parts24)
    beside = beside0 + beside1
    parts3 = exchanged(summed_parts([(3, beside_tile)], [beside], np.array([1])))
    (ready,) = call(
        functools.partial(add_kernel, sizes[4]),
        0, [(slots * sizes[3], WIN, part, size)], [], 10**6, *parts24, *parts3,
    )
    got = lax.all_to_all(ready, ("zh", "zl"), 0, 0)
    piece = part // slots
    sent = call(
        functools.partial(finish_kernel, factor),
        1, [(WIN, piece, size)] * 2, [pltpu.VMEM((WIN, part, size), F32)], 3 * 6 * part * size**2,
        place, got, whole,
    )

    def sent_to(flip):
        def target(y, c, zh, zl, x):
            r = (y * sizes[1] + c - 2) % rows_count
            pick = zh if flip == 0 else 1 - zh
            n = 2 * (x * sizes[3] + zl) + pick
            return r // sizes[1], r % sizes[1], n // (sizes[3] * sizes[4]), n // sizes[4] % sizes[3], n % sizes[4]
        return target

    back = [lax.ppermute(sent[flip], AXES, pairs_of(sizes, sent_to(flip))) for flip in range(2)]
    swap = (col % 2 == 1) ^ (row >= rows_count - 2)
    low = jnp.where(swap, back[1], back[0])
    high = jnp.where(swap, back[0], back[1])
    return jnp.stack([low, high], 1)[:, :, None]


def solution(mesh):
    sizes = (mesh.shape["row"] // 2, 2, 2, mesh.shape["col"] // 8, 4)
    fine = Mesh(mesh.devices.reshape(sizes), AXES)
    rows, cols = AXES[:2], AXES[2:]
    placed = (P(None, rows, None, cols, None, None), P(None, rows, None, cols, None, None), P())
    return jax.shard_map(
        lambda *args: on_device(sizes, *args),
        mesh=fine,
        in_specs=placed,
        out_specs=P(None, None, rows, cols, None),
        check_vma=False,
    )
```

```python
import functools
import math

import jax
import jax.numpy as jnp
import numpy as np
from jax import lax
from jax.experimental import pallas as pl
from jax.experimental.pallas import tpu as pltpu
from jax.sharding import Mesh, PartitionSpec as P

TOP = 4
WIN = 3
AXES = ("y", "core", "zh", "zl", "x")
F32 = jnp.float32


def pairs_of(sizes, target):
    pairs = []
    for number in range(math.prod(sizes)):
        there = target(*(int(i) for i in np.unravel_index(number, sizes)))
        if there is not None:
            pairs.append((number, int(np.ravel_multi_index(there, sizes))))
    return pairs


def halves(x):
    high = x.astype(jnp.bfloat16)
    return high, (x - high.astype(F32)).astype(jnp.bfloat16)


def times(a, b):
    dims = (((1,), (1,)), ((), ()))
    dot = functools.partial(lax.dot_general, dimension_numbers=dims, preferred_element_type=F32)
    return dot(a[0], b[0]) + (dot(a[0], b[1]) + dot(a[1], b[0]))


def product_kernel(tile_count, factor, place, left_ref, home_ref, ahead_ref, beside0_ref, beside1_ref, row_codes, col_codes, out):
    row, col, core = place[0], place[1], place[3]
    slots, size = left_ref.shape[0], left_ref.shape[1]
    rows_count = tile_count // slots
    block = size // out.shape[0]
    gap = lax.broadcasted_iota(jnp.int32, (size, size), 1) - lax.broadcasted_iota(jnp.int32, (size, size), 0)
    for slot in range(slots):
        other = slots - 1 - slot
        tile_row = slot * rows_count + row - 2
        left = left_ref[jnp.where(row < 2, 0, slot)]
        left_halves = halves(left)
        live = (tile_row >= 0) & (col > tile_row + TOP)
        scale = jnp.where(live, factor, 0.0).astype(F32)
        for number in range(WIN):
            e = TOP - number
            if e == 4:
                tile = ahead_ref[jnp.where(row >= rows_count - 2, other, slot)]
            elif e == 3:
                after = beside1_ref[jnp.where(row >= rows_count - 1, other, slot)]
                tile = jnp.where(core == 0, beside0_ref[slot], after)
            else:
                tile = home_ref[slot]
            total = row_codes[number, slot] + col_codes[...]
            allowed = ((total == 3) | (total == 5)) & (gap + (col - tile_row - e) * size > 3)
            right = halves(jnp.where(allowed, tile, 0.0))
            own = jnp.where((tile_row >= 0) & (col == tile_row + e), 1.0, 0.0).astype(F32)
            full = scale * times(left_halves, right) + own * left
            for x in range(out.shape[0]):
                out[x, number, slot] = full[x * block:(x + 1) * block]


def add_kernel(got, out):
    slots, rows = got.shape[2:4]
    deep = out.shape[0] // slots
    piece = rows // deep
    for number in range(WIN):
        for slot in range(slots):
            total = got[0, number, slot]
            for k in range(1, got.shape[0]):
                total = total + got[k, number, slot]
            for z in range(deep):
                out[slot * deep + z, number] = total[z * piece:(z + 1) * piece]


def finish_kernel(factor, place, got, *refs):
    packs, out_a, out_b, whole, rows = refs[:-4], refs[-4], refs[-3], refs[-2], refs[-1]
    half, x, zl = place[2], place[4], place[5]
    deep, _, part, _ = packs[0].shape
    for j, pack in enumerate(packs):
        for i in range(deep):
            start = pl.multiple_of(((zl ^ i) * len(packs) + (x ^ j)) * part, part)
            for k in range(3):
                whole[k, pl.ds(start, part), :] = pack[i, k]
    sums = []
    for w in range(WIN):
        total = got[0, w]
        for k in range(1, got.shape[0]):
            total = total + got[k, w]
        sums.append(total)
    w4 = sums[0]
    w4_halves = halves(w4)
    w3 = sums[1] + factor * times(w4_halves, halves(whole[2]))
    w2 = sums[2] + factor * (times(w4_halves, halves(whole[1])) + times(halves(w3), halves(whole[0])))
    piece = out_a.shape[1]
    for w, value in enumerate((w4, w3, w2)):
        rows[w] = value
        out_a[w] = rows[w, pl.ds(pl.multiple_of(half * piece, piece), piece), :]
        out_b[w] = rows[w, pl.ds(pl.multiple_of((1 - half) * piece, piece), piece), :]


def call(kernel, in_count, outs, scratch, flops, *args):
    spec = pl.BlockSpec(memory_space=pltpu.VMEM)
    moved = sum(math.prod(a.shape) * 4 for a in args) + sum(math.prod(s) * 4 for s in outs)
    return pl.pallas_call(
        kernel,
        out_shape=[jax.ShapeDtypeStruct(s, F32) for s in outs],
        in_specs=[pl.BlockSpec(memory_space=pltpu.SMEM)] * in_count + [spec] * (len(args) - in_count),
        out_specs=[spec] * len(outs),
        scratch_shapes=scratch,
        cost_estimate=pl.CostEstimate(flops=flops, bytes_accessed=moved, transcendentals=0),
        compiler_params=pltpu.CompilerParams(vmem_limit_bytes=24 * 1024 * 1024),
    )(*args)


def on_device(sizes, inside, outer, sequence):
    rows_count = sizes[0] * sizes[1]
    cols_count = sizes[2] * sizes[3] * sizes[4]
    size = inside.shape[-1]
    slots = inside.shape[0]
    tile_count = slots * rows_count
    part = slots * size // cols_count
    factor = 1.0 / math.sqrt(tile_count)
    core = lax.axis_index("core")
    row = lax.axis_index("y") * sizes[1] + core
    half = lax.axis_index("zh")
    col = lax.axis_index(AXES[2:])
    place = jnp.stack([row, col, half, core, lax.axis_index("x"), lax.axis_index("zl")]).astype(jnp.int32)
    home = inside[:, 0, 0, 0]
    out_tiles = outer[:, 0, 0, 0]

    def row_shift(v, by):
        n = sizes[0]
        return lax.ppermute(v, "y", [(i, (i + by) % n) for i in range(n)])

    left = row_shift(out_tiles, 1)
    ahead = row_shift(home, -1)
    beside0 = lax.ppermute(home, "core", [(1, 0)])
    beside1 = lax.ppermute(ahead, "core", [(0, 1)])

    slot = jnp.arange(slots, dtype=jnp.int32)
    codes = sequence.reshape(tile_count, size)
    offsets = jnp.arange(size, dtype=jnp.int32)
    col_codes = lax.dynamic_index_in_dim(codes, col, 0, True)
    col_pos = col * size + offsets
    wanted = slot[None, :] * rows_count + row + (WIN - 1) - jnp.arange(WIN, dtype=jnp.int32)[:, None]
    row_codes = jnp.take(codes, jnp.clip(wanted, 0, tile_count - 1), axis=0)

    gap = col - row
    early = (gap == 1) | (gap == 2)
    near_row = jnp.where(early, row, rows_count + row)
    near_codes = jnp.where(early, row_codes[WIN - 1, 0], row_codes[WIN - 1, 1])
    total = near_codes[:, None] + col_codes
    far = col_pos[None, :] - (near_row * size + offsets)[:, None] > 3
    near = jnp.where(((total == 3) | (total == 5)) & far, jnp.where(early, home[0], home[1]), 0.0)
    near = near.reshape(1, size // part, part, size)
    spread = jnp.broadcast_to(near, (slots,) + near.shape[1:]).reshape(cols_count, part, size)
    spread = lax.all_to_all(spread, AXES[2:], 0, 0)
    first = jnp.minimum(row + half * rows_count + 1, cols_count - 1)
    second = jnp.minimum(row + half * rows_count + 2, cols_count - 1)
    near1 = lax.dynamic_index_in_dim(spread, first, 0, False)
    near2 = lax.dynamic_index_in_dim(spread, second, 0, False)
    near1, near2, left, ahead = lax.optimization_barrier((near1, near2, left, ahead))

    def previous_row(y, c, zh, zl, x):
        r = y * sizes[1] + c
        zh = zh if r > 0 else (zh + 1) % sizes[2]
        r = (r - 1) % rows_count
        return r // sizes[1], r % sizes[1], zh, zl, x

    next1 = lax.ppermute(near1, AXES, pairs_of(sizes, previous_row))
    bits = jnp.stack([near1, near2, next1])

    def partners(v, axis, n):
        return [v] + [lax.ppermute(v, axis, [(i, i ^ j) for i in range(n)]) for j in range(1, n)]

    packs = partners(jnp.stack(partners(bits, "zl", sizes[3])), "x", sizes[4])

    wide = (sizes[4], WIN, slots, size // sizes[4], size)
    (parts,) = call(
        functools.partial(product_kernel, tile_count, factor),
        1, [wide], [], WIN * slots * 6 * size**3,
        place, left, home, ahead, beside0, beside1, row_codes[..., None], col_codes,
    )
    parts = lax.all_to_all(parts, "x", 0, 0)
    (ready,) = call(add_kernel, 0, [(slots * sizes[3], WIN, part, size)], [], 10**6, parts)
    got = lax.all_to_all(ready, ("zh", "zl"), 0, 0)
    piece = part // slots
    sent = call(
        functools.partial(finish_kernel, factor),
        1, [(WIN, piece, size)] * 2, [pltpu.VMEM((3, size, size), F32), pltpu.VMEM((WIN, part, size), F32)],
        3 * 6 * part * size**2, place, got, *packs,
    )

    def sent_to(flip):
        def target(y, c, zh, zl, x):
            r = (y * sizes[1] + c - 2) % rows_count
            pick = zh if flip == 0 else 1 - zh
            n = 2 * (x * sizes[3] + zl) + pick
            return r // sizes[1], r % sizes[1], n // (sizes[3] * sizes[4]), n // sizes[4] % sizes[3], n % sizes[4]
        return target

    back = [lax.ppermute(sent[flip], AXES, pairs_of(sizes, sent_to(flip))) for flip in range(2)]
    swap = (col % 2 == 1) ^ (row >= rows_count - 2)
    low = jnp.where(swap, back[1], back[0])
    high = jnp.where(swap, back[0], back[1])
    return jnp.stack([low, high], 1)[:, :, None]


def solution(mesh):
    sizes = (mesh.shape["row"] // 2, 2, 2, mesh.shape["col"] // 8, 4)
    fine = Mesh(mesh.devices.reshape(sizes), AXES)
    rows, cols = AXES[:2], AXES[2:]
    placed = (P(None, rows, None, cols, None, None), P(None, rows, None, cols, None, None), P())
    return jax.shard_map(
        lambda *args: on_device(sizes, *args),
        mesh=fine,
        in_specs=placed,
        out_specs=P(None, None, rows, cols, None),
        check_vma=False,
    )
```

```python
import functools
import math

import jax
import jax.numpy as jnp
import numpy as np
from jax import lax
from jax.experimental import pallas as pl
from jax.experimental.pallas import tpu as pltpu
from jax.sharding import Mesh, PartitionSpec as P

TOP = 4
WIN = 3
AXES = ("y", "core", "zh", "zl", "x")
F32 = jnp.float32


def pairs_of(sizes, target):
    pairs = []
    for number in range(math.prod(sizes)):
        there = target(*(int(i) for i in np.unravel_index(number, sizes)))
        if there is not None:
            pairs.append((number, int(np.ravel_multi_index(there, sizes))))
    return pairs


def halves(x):
    high = x.astype(jnp.bfloat16)
    return high, (x - high.astype(F32)).astype(jnp.bfloat16)


def times(a, b):
    dims = (((1,), (1,)), ((), ()))
    dot = functools.partial(lax.dot_general, dimension_numbers=dims, preferred_element_type=F32)
    return dot(a[0], b[0]) + (dot(a[0], b[1]) + dot(a[1], b[0]))


def codes_of(codes, tile):
    return codes[pl.ds(jnp.clip(tile, 0, codes.shape[0] - 1), 1), :].astype(F32)


def down(values):
    size = values.shape[1]
    return jnp.broadcast_to(values, (size, size)).T


def masked(tile, total, gap):
    return jnp.where(((total == 3.0) | (total == 5.0)) & (gap > 3), tile, 0.0)


def product_kernel(factor, place, left_ref, home_ref, ahead_ref, beside0_ref, beside1_ref, codes, out):
    row, col, core = place[0], place[1], place[3]
    slots, size = left_ref.shape[0], left_ref.shape[1]
    rows_count = codes.shape[0] // slots
    block = size // out.shape[0]
    col_codes = codes_of(codes, col)
    gap = lax.broadcasted_iota(jnp.int32, (size, size), 1) - lax.broadcasted_iota(jnp.int32, (size, size), 0)
    for slot in range(slots):
        other = slots - 1 - slot
        tile_row = slot * rows_count + row - 2
        left = left_ref[jnp.where(row < 2, 0, slot)]
        left_halves = halves(left)
        live = (tile_row >= 0) & (col > tile_row + TOP)
        scale = jnp.where(live, factor, 0.0).astype(F32)
        for number in range(WIN):
            e = TOP - number
            if e == 4:
                tile = ahead_ref[jnp.where(row >= rows_count - 2, other, slot)]
            elif e == 3:
                after = beside1_ref[jnp.where(row >= rows_count - 1, other, slot)]
                tile = jnp.where(core == 0, beside0_ref[slot], after)
            else:
                tile = home_ref[slot]
            total = down(codes_of(codes, tile_row + e)) + col_codes
            right = halves(masked(tile, total, gap + (col - tile_row - e) * size))
            own = jnp.where((tile_row >= 0) & (col == tile_row + e), 1.0, 0.0).astype(F32)
            full = scale * times(left_halves, right) + own * left
            for x in range(out.shape[0]):
                out[x, number, slot] = full[x * block:(x + 1) * block]


def add_kernel(got, out):
    slots, rows = got.shape[2:4]
    deep = out.shape[0] // slots
    piece = rows // deep
    for number in range(WIN):
        for slot in range(slots):
            total = got[0, number, slot]
            for k in range(1, got.shape[0]):
                total = total + got[k, number, slot]
            for z in range(deep):
                out[slot * deep + z, number] = total[z * piece:(z + 1) * piece]


def pack_kernel(wide, place, codes, *refs):
    bits, out, columns = refs[:-2], refs[-2], refs[-1]
    row, half, x, zl = place[0], place[2], place[4], place[5]
    part, size = out.shape[2:]
    first = row + half * (codes.shape[0] // 2)
    for k, (at, beyond) in enumerate(((0, 1), (0, 2), (1, 1))):
        columns[...] = down(codes_of(codes, first + at))
        lanes = codes_of(codes, first + at + beyond)
        for i, ref in enumerate(bits):
            start = pl.multiple_of(((zl ^ i) * wide + x) * part, part)
            total = columns[pl.ds(start, part), :] + lanes
            steps = lax.broadcasted_iota(jnp.int32, (part, size), 1) - lax.broadcasted_iota(jnp.int32, (part, size), 0)
            out[i, k] = masked(ref[k], total, steps - start + beyond * size)


def finish_kernel(factor, place, got, *refs):
    packs, out_a, out_b, whole, rows = refs[:-4], refs[-4], refs[-3], refs[-2], refs[-1]
    half, x, zl = place[2], place[4], place[5]
    deep, _, part, _ = packs[0].shape
    for j, pack in enumerate(packs):
        for i in range(deep):
            start = pl.multiple_of(((zl ^ i) * len(packs) + (x ^ j)) * part, part)
            for k in range(3):
                whole[k, pl.ds(start, part), :] = pack[i, k]
    sums = []
    for w in range(WIN):
        total = got[0, w]
        for k in range(1, got.shape[0]):
            total = total + got[k, w]
        sums.append(total)
    w4 = sums[0]
    w4_halves = halves(w4)
    w3 = sums[1] + factor * times(w4_halves, halves(whole[2]))
    w2 = sums[2] + factor * (times(w4_halves, halves(whole[1])) + times(halves(w3), halves(whole[0])))
    piece = out_a.shape[1]
    for w, value in enumerate((w4, w3, w2)):
        rows[w] = value
        out_a[w] = rows[w, pl.ds(pl.multiple_of(half * piece, piece), piece), :]
        out_b[w] = rows[w, pl.ds(pl.multiple_of((1 - half) * piece, piece), piece), :]


def call(kernel, in_count, outs, scratch, flops, *args):
    spec = pl.BlockSpec(memory_space=pltpu.VMEM)
    moved = sum(math.prod(a.shape) * 4 for a in args) + sum(math.prod(s) * 4 for s in outs)
    return pl.pallas_call(
        kernel,
        out_shape=[jax.ShapeDtypeStruct(s, F32) for s in outs],
        in_specs=[pl.BlockSpec(memory_space=pltpu.SMEM)] * in_count + [spec] * (len(args) - in_count),
        out_specs=[spec] * len(outs),
        scratch_shapes=scratch,
        cost_estimate=pl.CostEstimate(flops=flops, bytes_accessed=moved, transcendentals=0),
        compiler_params=pltpu.CompilerParams(vmem_limit_bytes=24 * 1024 * 1024),
    )(*args)


def on_device(sizes, inside, outer, sequence):
    rows_count = sizes[0] * sizes[1]
    cols_count = sizes[2] * sizes[3] * sizes[4]
    size = inside.shape[-1]
    slots = inside.shape[0]
    tile_count = slots * rows_count
    part = slots * size // cols_count
    factor = 1.0 / math.sqrt(tile_count)
    core = lax.axis_index("core")
    row = lax.axis_index("y") * sizes[1] + core
    half = lax.axis_index("zh")
    col = lax.axis_index(AXES[2:])
    place = jnp.stack([row, col, half, core, lax.axis_index("x"), lax.axis_index("zl")]).astype(jnp.int32)
    home = inside[:, 0, 0, 0]
    out_tiles = outer[:, 0, 0, 0]

    def row_shift(v, by):
        n = sizes[0]
        return lax.ppermute(v, "y", [(i, (i + by) % n) for i in range(n)])

    left = row_shift(out_tiles, 1)
    ahead = row_shift(home, -1)
    beside0 = lax.ppermute(home, "core", [(1, 0)])
    beside1 = lax.ppermute(ahead, "core", [(0, 1)])

    codes = sequence.reshape(tile_count, size)

    spread, beside0 = lax.optimization_barrier((home.reshape(cols_count, part, size), beside0))
    spread = lax.all_to_all(spread, AXES[2:], 0, 0)
    first = jnp.minimum(row + half * rows_count + 1, cols_count - 1)
    second = jnp.minimum(row + half * rows_count + 2, cols_count - 1)
    near1 = lax.dynamic_index_in_dim(spread, first, 0, False)
    near2 = lax.dynamic_index_in_dim(spread, second, 0, False)

    def previous_row(y, c, zh, zl, x):
        r = y * sizes[1] + c
        zh = zh if r > 0 else (zh + 1) % sizes[2]
        r = (r - 1) % rows_count
        return r // sizes[1], r % sizes[1], zh, zl, x

    next1 = lax.ppermute(near1, AXES, pairs_of(sizes, previous_row))
    bits = jnp.stack([near1, near2, next1])

    def partners(v, axis, n):
        return [v] + [lax.ppermute(v, axis, [(i, i ^ j) for i in range(n)]) for j in range(1, n)]

    (pack,) = call(
        functools.partial(pack_kernel, sizes[4]),
        1, [(sizes[3], 3, part, size)], [pltpu.VMEM((size, size), F32)], 10**6,
        place, codes, *partners(bits, "zl", sizes[3]),
    )

    wide = (sizes[4], WIN, slots, size // sizes[4], size)
    (parts,) = call(
        functools.partial(product_kernel, factor),
        1, [wide], [], WIN * slots * 6 * size**3,
        place, left, home, ahead, beside0, beside1, codes,
    )
    parts = lax.all_to_all(parts, "x", 0, 0)
    parts, pack = lax.optimization_barrier((parts, pack))
    packs = partners(pack, "x", sizes[4])
    (ready,) = call(add_kernel, 0, [(slots * sizes[3], WIN, part, size)], [], 10**6, parts)
    got = lax.all_to_all(ready, ("zh", "zl"), 0, 0)
    piece = part // slots
    sent = call(
        functools.partial(finish_kernel, factor),
        1, [(WIN, piece, size)] * 2, [pltpu.VMEM((3, size, size), F32), pltpu.VMEM((WIN, part, size), F32)],
        3 * 6 * part * size**2, place, got, *packs,
    )

    def sent_to(flip):
        def target(y, c, zh, zl, x):
            r = (y * sizes[1] + c - 2) % rows_count
            pick = zh if flip == 0 else 1 - zh
            n = 2 * (x * sizes[3] + zl) + pick
            return r // sizes[1], r % sizes[1], n // (sizes[3] * sizes[4]), n // sizes[4] % sizes[3], n % sizes[4]
        return target

    back = [lax.ppermute(sent[flip], AXES, pairs_of(sizes, sent_to(flip))) for flip in range(2)]
    swap = (col % 2 == 1) ^ (row >= rows_count - 2)
    low = jnp.where(swap, back[1], back[0])
    high = jnp.where(swap, back[0], back[1])
    return jnp.stack([low, high], 1)[:, :, None]


def solution(mesh):
    sizes = (mesh.shape["row"] // 2, 2, 2, mesh.shape["col"] // 8, 4)
    fine = Mesh(mesh.devices.reshape(sizes), AXES)
    rows, cols = AXES[:2], AXES[2:]
    placed = (P(None, rows, None, cols, None, None), P(None, rows, None, cols, None, None), P())
    return jax.shard_map(
        lambda *args: on_device(sizes, *args),
        mesh=fine,
        in_specs=placed,
        out_specs=P(None, None, rows, cols, None),
        check_vma=False,
    )
```

```python
import functools
import math

import jax
import jax.numpy as jnp
import numpy as np
from jax import lax
from jax.experimental import pallas as pl
from jax.experimental.pallas import tpu as pltpu
from jax.sharding import Mesh, PartitionSpec as P

TOP = 4
WIN = 3
AXES = ("y", "core", "zh", "zl", "x")
F32 = jnp.float32


def pairs_of(sizes, target):
    pairs = []
    for number in range(math.prod(sizes)):
        there = target(*(int(i) for i in np.unravel_index(number, sizes)))
        if there is not None:
            pairs.append((number, int(np.ravel_multi_index(there, sizes))))
    return pairs


def halves(x):
    high = x.astype(jnp.bfloat16)
    return high, (x - high.astype(F32)).astype(jnp.bfloat16)


def times(a, b):
    dims = (((1,), (1,)), ((), ()))
    dot = functools.partial(lax.dot_general, dimension_numbers=dims, preferred_element_type=F32)
    return dot(a[0], b[0]) + (dot(a[0], b[1]) + dot(a[1], b[0]))


def codes_of(codes, tile):
    return codes[pl.ds(jnp.clip(tile, 0, codes.shape[0] - 1), 1), :]


def columns_of(codes, tiles):
    total = codes_of(codes, tiles[0])
    for k, tile in enumerate(tiles[1:], 1):
        total = total + (codes_of(codes, tile) << (2 * k))
    size = codes.shape[1]
    return jnp.broadcast_to(total, (size, size)).T


def masked(tile, total, gap):
    return jnp.where(((total == 3) | (total == 5)) & (gap > 3), tile, 0.0)


def product_kernel(factor, place, left_ref, ahead_ref, beside0_ref, beside1_ref, codes, home_ref, out):
    row, col, core = place[0], place[1], place[3]
    slots, size = left_ref.shape[0], left_ref.shape[1]
    rows_count = codes.shape[0] // slots
    block = size // out.shape[0]
    col_codes = codes_of(codes, col)
    tile_rows = [slot * rows_count + row - 2 for slot in range(slots)]
    keys = [(slot, e) for e in (4, 3, 2) for slot in range(slots)]
    columns = columns_of(codes, [tile_rows[slot] + e for slot, e in keys])
    gap = lax.broadcasted_iota(jnp.int32, (size, size), 1) - lax.broadcasted_iota(jnp.int32, (size, size), 0)
    lefts = [left_ref[jnp.where(row < 2, 0, slot)] for slot in range(slots)]
    left_halves = [halves(left) for left in lefts]
    for k, (slot, e) in enumerate(keys):
        tile_row = tile_rows[slot]
        other = slots - 1 - slot
        if e == 4:
            tile = ahead_ref[jnp.where(row >= rows_count - 2, other, slot)]
        elif e == 3:
            after = beside1_ref[jnp.where(row >= rows_count - 1, other, slot)]
            tile = jnp.where(core == 0, beside0_ref[slot], after)
        else:
            tile = home_ref[slot]
        total = ((columns >> (2 * k)) & 3) + col_codes
        right = halves(masked(tile, total, gap + (col - tile_row - e) * size))
        live = (tile_row >= 0) & (col > tile_row + TOP)
        scale = jnp.where(live, factor, 0.0).astype(F32)
        own = jnp.where((tile_row >= 0) & (col == tile_row + e), 1.0, 0.0).astype(F32)
        full = scale * times(left_halves[slot], right) + own * lefts[slot]
        for x in range(out.shape[0]):
            out[x, TOP - e, slot] = full[x * block:(x + 1) * block]


def add_kernel(got, out):
    slots, rows = got.shape[2:4]
    deep = out.shape[0] // slots
    piece = rows // deep
    for number in range(WIN):
        for slot in range(slots):
            total = got[0, number, slot]
            for k in range(1, got.shape[0]):
                total = total + got[k, number, slot]
            for z in range(deep):
                out[slot * deep + z, number] = total[z * piece:(z + 1) * piece]


def pack_kernel(wide, place, codes, bits0, bits1, bits2, out, columns):
    row, half, x, zl = place[0], place[2], place[4], place[5]
    part, size = out.shape[2:]
    first = row + half * (codes.shape[0] // 2)
    columns[...] = columns_of(codes, [first, first + 1])
    steps = lax.broadcasted_iota(jnp.int32, (part, size), 1) - lax.broadcasted_iota(jnp.int32, (part, size), 0)
    for i in range(out.shape[0]):
        start = pl.multiple_of(((zl ^ i) * wide + x) * part, part)
        down = columns[pl.ds(start, part), :]
        for k, (at, beyond) in enumerate(((0, 1), (0, 2), (1, 1))):
            piece = bits0[k] if i == 0 else bits1[k] if i == 1 else bits2[i - 2, k]
            total = ((down >> (2 * at)) & 3) + codes_of(codes, first + at + beyond)
            out[i, k] = masked(piece, total, steps - start + beyond * size)


def finish_kernel(factor, place, got, *refs):
    packs, out_a, out_b, whole, rows = refs[:-4], refs[-4], refs[-3], refs[-2], refs[-1]
    half, x, zl = place[2], place[4], place[5]
    deep, _, part, _ = packs[0].shape
    for j, pack in enumerate(packs):
        for i in range(deep):
            start = pl.multiple_of(((zl ^ i) * len(packs) + (x ^ j)) * part, part)
            for k in range(3):
                whole[k, pl.ds(start, part), :] = pack[i, k]
    sums = []
    for w in range(WIN):
        total = got[0, w]
        for k in range(1, got.shape[0]):
            total = total + got[k, w]
        sums.append(total)
    w4 = sums[0]
    w4_halves = halves(w4)
    w3 = sums[1] + factor * times(w4_halves, halves(whole[2]))
    w2 = sums[2] + factor * (times(w4_halves, halves(whole[1])) + times(halves(w3), halves(whole[0])))
    piece = out_a.shape[1]
    for w, value in enumerate((w4, w3, w2)):
        rows[w] = value
        out_a[w] = rows[w, pl.ds(pl.multiple_of(half * piece, piece), piece), :]
        out_b[w] = rows[w, pl.ds(pl.multiple_of((1 - half) * piece, piece), piece), :]


def order_kernel(place, back0, back1, out):
    swap = (place[1] + place[6]) % 2 == 1
    out[:, 0] = jnp.where(swap, back1[...], back0[...])
    out[:, 1] = jnp.where(swap, back0[...], back1[...])


def call(kernel, in_count, outs, scratch, flops, *args):
    spec = pl.BlockSpec(memory_space=pltpu.VMEM)
    moved = sum(math.prod(a.shape) * 4 for a in args) + sum(math.prod(s) * 4 for s in outs)
    return pl.pallas_call(
        kernel,
        out_shape=[jax.ShapeDtypeStruct(s, F32) for s in outs],
        in_specs=[pl.BlockSpec(memory_space=pltpu.SMEM)] * in_count + [spec] * (len(args) - in_count),
        out_specs=[spec] * len(outs),
        scratch_shapes=scratch,
        cost_estimate=pl.CostEstimate(flops=flops, bytes_accessed=moved, transcendentals=0),
        compiler_params=pltpu.CompilerParams(vmem_limit_bytes=24 * 1024 * 1024),
    )(*args)


def on_device(sizes, inside, outer, sequence):
    rows_count = sizes[0] * sizes[1]
    cols_count = sizes[2] * sizes[3] * sizes[4]
    size = inside.shape[-1]
    slots = inside.shape[0]
    tile_count = slots * rows_count
    part = slots * size // cols_count
    factor = 1.0 / math.sqrt(tile_count)
    core = lax.axis_index("core")
    row = lax.axis_index("y") * sizes[1] + core
    half = lax.axis_index("zh")
    col = lax.axis_index(AXES[2:])
    late = (row >= rows_count - 2).astype(jnp.int32)
    place = jnp.stack([row, col, half, core, lax.axis_index("x"), lax.axis_index("zl"), late]).astype(jnp.int32)
    home = inside[:, 0, 0, 0]
    out_tiles = outer[:, 0, 0, 0]

    def row_shift(v, by):
        n = sizes[0]
        return lax.ppermute(v, "y", [(i, (i + by) % n) for i in range(n)])

    left = row_shift(out_tiles, 1)
    ahead = row_shift(home, -1)
    beside0 = lax.ppermute(home, "core", [(1, 0)])
    left, ahead = lax.optimization_barrier((left, ahead))
    beside1 = lax.ppermute(ahead, "core", [(0, 1)])

    codes = sequence.reshape(tile_count, size)

    spread, beside0 = lax.optimization_barrier((home.reshape(cols_count, part, size), beside0))
    spread = lax.all_to_all(spread, AXES[2:], 0, 0)
    first = jnp.minimum(row + half * rows_count + 1, cols_count - 1)
    second = jnp.minimum(row + half * rows_count + 2, cols_count - 1)
    near1 = lax.dynamic_index_in_dim(spread, first, 0, False)
    near2 = lax.dynamic_index_in_dim(spread, second, 0, False)

    def previous_row(y, c, zh, zl, x):
        r = y * sizes[1] + c
        zh = zh if r > 0 else (zh + 1) % sizes[2]
        r = (r - 1) % rows_count
        return r // sizes[1], r % sizes[1], zh, zl, x

    next1 = lax.ppermute(near1, AXES, pairs_of(sizes, previous_row))

    def partner(v, axis, n, j):
        return lax.ppermute(v, axis, [(i, i ^ j) for i in range(n)])

    wide = (sizes[4], WIN, slots, size // sizes[4], size)
    (parts,) = call(
        functools.partial(product_kernel, factor),
        1, [wide], [], WIN * slots * 6 * size**3,
        place, left, ahead, beside0, beside1, codes, home,
    )
    bits0 = jnp.stack([near1, near2, next1])
    bits1 = partner(bits0, "zl", sizes[3], 1)
    bits2 = partner(jnp.stack([bits0, bits1]), "zl", sizes[3], 2)
    (pack,) = call(
        functools.partial(pack_kernel, sizes[4]),
        1, [(sizes[3], 3, part, size)], [pltpu.VMEM((size, size), jnp.int32)], 10**6,
        place, codes, bits0, bits1, bits2,
    )
    packs = [pack] + [partner(pack, "x", sizes[4], j) for j in range(1, sizes[4])]
    parts = lax.all_to_all(parts, "x", 0, 0)
    parts, _ = lax.optimization_barrier((parts, pack))
    (ready,) = call(add_kernel, 0, [(slots * sizes[3], WIN, part, size)], [], 10**6, parts)
    got = lax.all_to_all(ready, ("zh", "zl"), 0, 0)
    piece = part // slots
    sent = call(
        functools.partial(finish_kernel, factor),
        1, [(WIN, piece, size)] * 2, [pltpu.VMEM((3, size, size), F32), pltpu.VMEM((WIN, part, size), F32)],
        3 * 6 * part * size**2, place, got, *packs,
    )

    def sent_to(flip):
        def target(y, c, zh, zl, x):
            r = (y * sizes[1] + c - 2) % rows_count
            pick = zh if flip == 0 else 1 - zh
            n = 2 * (x * sizes[3] + zl) + pick
            return r // sizes[1], r % sizes[1], n // (sizes[3] * sizes[4]), n // sizes[4] % sizes[3], n % sizes[4]
        return target

    back = [lax.ppermute(sent[flip], AXES, pairs_of(sizes, sent_to(flip))) for flip in range(2)]
    (result,) = call(order_kernel, 1, [(WIN, slots, piece, size)], [], 10**4, place, *back)
    return result[:, :, None]


def solution(mesh):
    sizes = (mesh.shape["row"] // 2, 2, 2, mesh.shape["col"] // 8, 4)
    fine = Mesh(mesh.devices.reshape(sizes), AXES)
    rows, cols = AXES[:2], AXES[2:]
    placed = (P(None, rows, None, cols, None, None), P(None, rows, None, cols, None, None), P())
    return jax.shard_map(
        lambda *args: on_device(sizes, *args),
        mesh=fine,
        in_specs=placed,
        out_specs=P(None, None, rows, cols, None),
        check_vma=False,
    )
```

```python
import functools
import math

import jax
import jax.numpy as jnp
import numpy as np
from jax import lax
from jax.experimental import pallas as pl
from jax.experimental.pallas import tpu as pltpu
from jax.sharding import Mesh, PartitionSpec as P

TOP = 4
WIN = 3
AXES = ("y", "core", "zh", "zl", "x")
F32 = jnp.float32


def pairs_of(sizes, target):
    pairs = []
    for number in range(math.prod(sizes)):
        there = target(*(int(i) for i in np.unravel_index(number, sizes)))
        if there is not None:
            pairs.append((number, int(np.ravel_multi_index(there, sizes))))
    return pairs


def halves(x):
    high = x.astype(jnp.bfloat16)
    return high, (x - high.astype(F32)).astype(jnp.bfloat16)


def times(a, b):
    dims = (((1,), (1,)), ((), ()))
    dot = functools.partial(lax.dot_general, dimension_numbers=dims, preferred_element_type=F32)
    return dot(a[0], b[0]) + (dot(a[0], b[1]) + dot(a[1], b[0]))


def codes_of(codes, tile):
    return codes[pl.ds(jnp.clip(tile, 0, codes.shape[0] - 1), 1), :]


def partners_of(code):
    return jnp.where(code == 0, 8, jnp.where(code == 1, 4, jnp.where(code == 2, 10, 5)))


def columns_of(codes, tiles):
    total = partners_of(codes_of(codes, tiles[0]))
    for k, tile in enumerate(tiles[1:], 1):
        total = total + (partners_of(codes_of(codes, tile)) << (4 * k))
    size = codes.shape[1]
    return jnp.broadcast_to(total, (size, size)).T


def product_kernel(factor, place, left_ref, ahead_ref, beside0_ref, beside1_ref, codes, home_ref, out):
    row, col, core = place[0], place[1], place[3]
    slots, size = left_ref.shape[0], left_ref.shape[1]
    rows_count = codes.shape[0] // slots
    block = out.shape[2]
    deep = size // block
    col_bits = 1 << codes_of(codes, col)
    tile_rows = [slot * rows_count + row - 2 for slot in range(slots)]
    keys = [(slot, e) for e in (4, 3, 2) for slot in range(slots)]
    columns = columns_of(codes, [tile_rows[slot] + e for slot, e in keys])
    gap = lax.broadcasted_iota(jnp.int32, (size, size), 1) - lax.broadcasted_iota(jnp.int32, (size, size), 0)
    lefts = [left_ref[jnp.where(row < 2, 0, slot)] for slot in range(slots)]
    left_halves = [halves(left) for left in lefts]
    for k, (slot, e) in enumerate(keys):
        tile_row = tile_rows[slot]
        other = slots - 1 - slot
        allowed = (columns & (col_bits << (4 * k))) != 0
        if e == 4:
            tile = ahead_ref[jnp.where(row >= rows_count - 2, other, slot)]
            allowed = allowed & (gap > 3 - (col - tile_row - e) * size)
        elif e == 3:
            after = beside1_ref[jnp.where(row >= rows_count - 1, other, slot)]
            tile = jnp.where(core == 0, beside0_ref[slot], after)
        else:
            tile = home_ref[slot]
        right = halves(jnp.where(allowed, tile, 0.0))
        live = (tile_row >= 0) & (col > tile_row + TOP)
        scale = jnp.where(live, factor, 0.0).astype(F32)
        own = jnp.where((tile_row >= 0) & (col == tile_row + e), 1.0, 0.0).astype(F32)
        full = scale * times(left_halves[slot], right) + own * lefts[slot]
        for q in range(deep):
            out[slot * deep + q, TOP - e] = full[q * block:(q + 1) * block]


def pack_kernel(wide, place, codes, bits0, bits1, bits2, out, columns):
    row, half, x, zl = place[0], place[2], place[4], place[5]
    part, size = out.shape[2:]
    first = row + half * (codes.shape[0] // 2)
    columns[...] = columns_of(codes, [first, first + 1])
    steps = lax.broadcasted_iota(jnp.int32, (part, size), 1) - lax.broadcasted_iota(jnp.int32, (part, size), 0)
    for i in range(out.shape[0]):
        start = pl.multiple_of(((zl ^ i) * wide + x) * part, part)
        down = columns[pl.ds(start, part), :]
        for k, (at, beyond) in enumerate(((0, 1), (0, 2), (1, 1))):
            piece = bits0[k] if i == 0 else bits1[k] if i == 1 else bits2[i - 2, k]
            allowed = (down & (1 << (codes_of(codes, first + at + beyond) + 4 * at))) != 0
            far = steps > 3 + start - beyond * size
            out[i, k] = jnp.where(allowed & far, piece, 0.0)


def finish_kernel(factor, place, got, *refs):
    packs, out_a, out_b, whole, rows = refs[:-4], refs[-4], refs[-3], refs[-2], refs[-1]
    half, x, zl = place[2], place[4], place[5]
    deep, _, part, _ = packs[0].shape
    for j, pack in enumerate(packs):
        for i in range(deep):
            start = pl.multiple_of(((zl ^ i) * len(packs) + (x ^ j)) * part, part)
            for k in range(3):
                whole[k, pl.ds(start, part), :] = pack[i, k]
    sums = []
    for w in range(WIN):
        total = got[0, w]
        for k in range(1, got.shape[0]):
            total = total + got[k, w]
        sums.append(total)
    w4 = sums[0]
    w4_halves = halves(w4)
    w3 = sums[1] + factor * times(w4_halves, halves(whole[2]))
    w2 = sums[2] + factor * (times(w4_halves, halves(whole[1])) + times(halves(w3), halves(whole[0])))
    piece = out_a.shape[1]
    for w, value in enumerate((w4, w3, w2)):
        rows[w] = value
        out_a[w] = rows[w, pl.ds(pl.multiple_of(half * piece, piece), piece), :]
        out_b[w] = rows[w, pl.ds(pl.multiple_of((1 - half) * piece, piece), piece), :]


def order_kernel(place, back0, back1, out):
    swap = (place[1] + place[6]) % 2 == 1
    out[:, 0] = jnp.where(swap, back1[...], back0[...])
    out[:, 1] = jnp.where(swap, back0[...], back1[...])


def call(kernel, in_count, outs, scratch, flops, *args):
    spec = pl.BlockSpec(memory_space=pltpu.VMEM)
    moved = sum(math.prod(a.shape) * 4 for a in args) + sum(math.prod(s) * 4 for s in outs)
    return pl.pallas_call(
        kernel,
        out_shape=[jax.ShapeDtypeStruct(s, F32) for s in outs],
        in_specs=[pl.BlockSpec(memory_space=pltpu.SMEM)] * in_count + [spec] * (len(args) - in_count),
        out_specs=[spec] * len(outs),
        scratch_shapes=scratch,
        cost_estimate=pl.CostEstimate(flops=flops, bytes_accessed=moved, transcendentals=0),
        compiler_params=pltpu.CompilerParams(vmem_limit_bytes=24 * 1024 * 1024),
    )(*args)


def on_device(sizes, inside, outer, sequence):
    rows_count = sizes[0] * sizes[1]
    cols_count = sizes[2] * sizes[3] * sizes[4]
    size = inside.shape[-1]
    slots = inside.shape[0]
    tile_count = slots * rows_count
    part = slots * size // cols_count
    factor = 1.0 / math.sqrt(tile_count)
    core = lax.axis_index("core")
    row = lax.axis_index("y") * sizes[1] + core
    half = lax.axis_index("zh")
    col = lax.axis_index(AXES[2:])
    late = (row >= rows_count - 2).astype(jnp.int32)
    place = jnp.stack([row, col, half, core, lax.axis_index("x"), lax.axis_index("zl"), late]).astype(jnp.int32)
    home = inside[:, 0, 0, 0]
    out_tiles = outer[:, 0, 0, 0]

    def row_shift(v, by):
        n = sizes[0]
        return lax.ppermute(v, "y", [(i, (i + by) % n) for i in range(n)])

    left = row_shift(out_tiles, 1)
    ahead = row_shift(home, -1)
    beside0 = lax.ppermute(home, "core", [(1, 0)])
    left, ahead = lax.optimization_barrier((left, ahead))
    beside1 = lax.ppermute(ahead, "core", [(0, 1)])

    codes = sequence.reshape(tile_count, size)

    spread, beside0 = lax.optimization_barrier((home.reshape(cols_count, part, size), beside0))
    spread = lax.all_to_all(spread, AXES[2:], 0, 0)
    first = jnp.minimum(row + half * rows_count + 1, cols_count - 1)
    second = jnp.minimum(row + half * rows_count + 2, cols_count - 1)
    near1 = lax.dynamic_index_in_dim(spread, first, 0, False)
    near2 = lax.dynamic_index_in_dim(spread, second, 0, False)

    def previous_row(y, c, zh, zl, x):
        r = y * sizes[1] + c
        zh = zh if r > 0 else (zh + 1) % sizes[2]
        r = (r - 1) % rows_count
        return r // sizes[1], r % sizes[1], zh, zl, x

    next1 = lax.ppermute(near1, AXES, pairs_of(sizes, previous_row))

    def partner(v, axis, n, j):
        return lax.ppermute(v, axis, [(i, i ^ j) for i in range(n)])

    (parts,) = call(
        functools.partial(product_kernel, factor),
        1, [(cols_count, WIN, part, size)], [], WIN * slots * 6 * size**3,
        place, left, ahead, beside0, beside1, codes, home,
    )
    bits0 = jnp.stack([near1, near2, next1])
    bits1 = partner(bits0, "zl", sizes[3], 1)
    bits2 = partner(jnp.stack([bits0, bits1]), "zl", sizes[3], 2)
    (pack,) = call(
        functools.partial(pack_kernel, sizes[4]),
        1, [(sizes[3], 3, part, size)], [pltpu.VMEM((size, size), jnp.int32)], 10**6,
        place, codes, bits0, bits1, bits2,
    )
    packs = [pack] + [partner(pack, "x", sizes[4], j) for j in range(1, sizes[4])]
    got = lax.all_to_all(parts, AXES[2:], 0, 0)
    piece = part // slots
    sent = call(
        functools.partial(finish_kernel, factor),
        1, [(WIN, piece, size)] * 2, [pltpu.VMEM((3, size, size), F32), pltpu.VMEM((WIN, part, size), F32)],
        3 * 6 * part * size**2, place, got, *packs,
    )

    def sent_to(flip):
        def target(y, c, zh, zl, x):
            r = (y * sizes[1] + c - 2) % rows_count
            pick = zh if flip == 0 else 1 - zh
            n = 2 * (zl * sizes[4] + x) + pick
            return r // sizes[1], r % sizes[1], n // (sizes[3] * sizes[4]), n // sizes[4] % sizes[3], n % sizes[4]
        return target

    back = [lax.ppermute(sent[flip], AXES, pairs_of(sizes, sent_to(flip))) for flip in range(2)]
    (result,) = call(order_kernel, 1, [(WIN, slots, piece, size)], [], 10**4, place, *back)
    return result[:, :, None]


def solution(mesh):
    sizes = (mesh.shape["row"] // 2, 2, 2, mesh.shape["col"] // 8, 4)
    fine = Mesh(mesh.devices.reshape(sizes), AXES)
    rows, cols = AXES[:2], AXES[2:]
    placed = (P(None, rows, None, cols, None, None), P(None, rows, None, cols, None, None), P())
    return jax.shard_map(
        lambda *args: on_device(sizes, *args),
        mesh=fine,
        in_specs=placed,
        out_specs=P(None, None, rows, cols, None),
        check_vma=False,
    )
```

```python
import functools
import math

import jax
import jax.numpy as jnp
import numpy as np
from jax import lax
from jax.experimental import pallas as pl
from jax.experimental.pallas import tpu as pltpu
from jax.sharding import Mesh, PartitionSpec as P

TOP = 4
WIN = 3
AXES = ("y", "core", "zh", "zl", "x")
F32 = jnp.float32


def pairs_of(sizes, target):
    pairs = []
    for number in range(math.prod(sizes)):
        there = target(*(int(i) for i in np.unravel_index(number, sizes)))
        if there is not None:
            pairs.append((number, int(np.ravel_multi_index(there, sizes))))
    return pairs


def halves(x):
    high = x.astype(jnp.bfloat16)
    return high, (x - high.astype(F32)).astype(jnp.bfloat16)


def times(a, b):
    dims = (((1,), (1,)), ((), ()))
    dot = functools.partial(lax.dot_general, dimension_numbers=dims, preferred_element_type=F32)
    return dot(a[0], b[0]) + (dot(a[0], b[1]) + dot(a[1], b[0]))


def codes_of(codes, tile):
    return codes[pl.ds(jnp.clip(tile, 0, codes.shape[0] - 1), 1), :]


def partners_of(code):
    return jnp.where(code == 0, 8, jnp.where(code == 1, 4, jnp.where(code == 2, 10, 5)))


def columns_of(codes, tiles):
    total = partners_of(codes_of(codes, tiles[0]))
    for k, tile in enumerate(tiles[1:], 1):
        total = total + (partners_of(codes_of(codes, tile)) << (4 * k))
    size = codes.shape[1]
    return jnp.broadcast_to(total, (size, size)).T


def product_kernel(factor, place, left_ref, ahead_ref, beside0_ref, beside1_ref, codes, home_ref, out):
    row, col, core = place[0], place[1], place[3]
    slots, size = left_ref.shape[0], left_ref.shape[1]
    rows_count = codes.shape[0] // slots
    block = size // out.shape[0]
    col_bits = 1 << codes_of(codes, col)
    tile_rows = [slot * rows_count + row - 2 for slot in range(slots)]
    keys = [(slot, e) for e in (4, 3, 2) for slot in range(slots)]
    columns = columns_of(codes, [tile_rows[slot] + e for slot, e in keys])
    gap = lax.broadcasted_iota(jnp.int32, (size, size), 1) - lax.broadcasted_iota(jnp.int32, (size, size), 0)
    lefts = [left_ref[jnp.where(row < 2, 0, slot)] for slot in range(slots)]
    left_halves = [halves(left) for left in lefts]
    for k, (slot, e) in enumerate(keys):
        tile_row = tile_rows[slot]
        other = slots - 1 - slot
        allowed = (columns & (col_bits << (4 * k))) != 0
        if e == 4:
            tile = ahead_ref[jnp.where(row >= rows_count - 2, other, slot)]
            allowed = allowed & (gap > 3 - (col - tile_row - e) * size)
        elif e == 3:
            after = beside1_ref[jnp.where(row >= rows_count - 1, other, slot)]
            tile = jnp.where(core == 0, beside0_ref[slot], after)
        else:
            tile = home_ref[slot]
        right = halves(jnp.where(allowed, tile, 0.0))
        live = (tile_row >= 0) & (col > tile_row + TOP)
        scale = jnp.where(live, factor, 0.0).astype(F32)
        own = jnp.where((tile_row >= 0) & (col == tile_row + e), 1.0, 0.0).astype(F32)
        full = scale * times(left_halves[slot], right) + own * lefts[slot]
        for x in range(out.shape[0]):
            out[x, TOP - e, slot] = full[x * block:(x + 1) * block]


def add_kernel(got, out):
    slots, rows = got.shape[2:4]
    deep = out.shape[0] // slots
    piece = rows // deep
    for number in range(WIN):
        for slot in range(slots):
            total = got[0, number, slot]
            for k in range(1, got.shape[0]):
                total = total + got[k, number, slot]
            for z in range(deep):
                out[slot * deep + z, number] = total[z * piece:(z + 1) * piece]


def pack_kernel(place, codes, gathered, next1, out, columns):
    row, half, zl = place[0], place[2], place[5]
    count, part, size = gathered.shape[0], gathered.shape[2], out.shape[2]
    first = row + half * (codes.shape[0] // 2)
    columns[...] = columns_of(codes, [first, first + 1])
    steps = lax.broadcasted_iota(jnp.int32, (part, size), 1) - lax.broadcasted_iota(jnp.int32, (part, size), 0)
    for i in range(count):
        start = pl.multiple_of((zl * count + i) * part, part)
        down = columns[pl.ds(start, part), :]
        for k, (at, beyond) in enumerate(((0, 1), (0, 2), (1, 1))):
            piece = gathered[i, k] if k < 2 else next1[i]
            allowed = (down & (1 << (codes_of(codes, first + at + beyond) + 4 * at))) != 0
            far = steps > 3 + start - beyond * size
            out[k, i * part:(i + 1) * part] = jnp.where(allowed & far, piece, 0.0)


def finish_kernel(factor, place, got, *refs):
    packs, out_a, out_b, whole, rows = refs[:-4], refs[-4], refs[-3], refs[-2], refs[-1]
    half, zl = place[2], place[5]
    rows_each = packs[0].shape[1]
    for j, pack in enumerate(packs):
        start = pl.multiple_of((zl ^ j) * rows_each, rows_each)
        for k in range(3):
            whole[k, pl.ds(start, rows_each), :] = pack[k]
    sums = []
    for w in range(WIN):
        total = got[0, w]
        for k in range(1, got.shape[0]):
            total = total + got[k, w]
        sums.append(total)
    w4 = sums[0]
    w4_halves = halves(w4)
    w3 = sums[1] + factor * times(w4_halves, halves(whole[2]))
    w2 = sums[2] + factor * (times(w4_halves, halves(whole[1])) + times(halves(w3), halves(whole[0])))
    piece = out_a.shape[1]
    for w, value in enumerate((w4, w3, w2)):
        rows[w] = value
        out_a[w] = rows[w, pl.ds(pl.multiple_of(half * piece, piece), piece), :]
        out_b[w] = rows[w, pl.ds(pl.multiple_of((1 - half) * piece, piece), piece), :]


def order_kernel(place, back0, back1, out):
    swap = (place[1] + place[6]) % 2 == 1
    out[:, 0] = jnp.where(swap, back1[...], back0[...])
    out[:, 1] = jnp.where(swap, back0[...], back1[...])


def call(kernel, in_count, outs, scratch, flops, *args):
    spec = pl.BlockSpec(memory_space=pltpu.VMEM)
    moved = sum(math.prod(a.shape) * 4 for a in args) + sum(math.prod(s) * 4 for s in outs)
    return pl.pallas_call(
        kernel,
        out_shape=[jax.ShapeDtypeStruct(s, F32) for s in outs],
        in_specs=[pl.BlockSpec(memory_space=pltpu.SMEM)] * in_count + [spec] * (len(args) - in_count),
        out_specs=[spec] * len(outs),
        scratch_shapes=scratch,
        cost_estimate=pl.CostEstimate(flops=flops, bytes_accessed=moved, transcendentals=0),
        compiler_params=pltpu.CompilerParams(vmem_limit_bytes=24 * 1024 * 1024),
    )(*args)


def on_device(sizes, inside, outer, sequence):
    rows_count = sizes[0] * sizes[1]
    cols_count = sizes[2] * sizes[3] * sizes[4]
    size = inside.shape[-1]
    slots = inside.shape[0]
    tile_count = slots * rows_count
    part = slots * size // cols_count
    factor = 1.0 / math.sqrt(tile_count)
    core = lax.axis_index("core")
    row = lax.axis_index("y") * sizes[1] + core
    half = lax.axis_index("zh")
    col = lax.axis_index(AXES[2:])
    late = (row >= rows_count - 2).astype(jnp.int32)
    place = jnp.stack([row, col, half, core, lax.axis_index("x"), lax.axis_index("zl"), late]).astype(jnp.int32)
    home = inside[:, 0, 0, 0]
    out_tiles = outer[:, 0, 0, 0]

    def row_shift(v, by):
        n = sizes[0]
        return lax.ppermute(v, "y", [(i, (i + by) % n) for i in range(n)])

    left = row_shift(out_tiles, 1)
    ahead = row_shift(home, -1)
    beside0 = lax.ppermute(home, "core", [(1, 0)])
    left, ahead = lax.optimization_barrier((left, ahead))
    beside1 = lax.ppermute(ahead, "core", [(0, 1)])

    codes = sequence.reshape(tile_count, size)

    spread = lax.all_to_all(home.reshape(cols_count, part, size), AXES[2:], 0, 0)
    first = jnp.minimum(row + half * rows_count + 1, cols_count - 1)
    second = jnp.minimum(row + half * rows_count + 2, cols_count - 1)
    near1 = lax.dynamic_index_in_dim(spread, first, 0, False)
    near2 = lax.dynamic_index_in_dim(spread, second, 0, False)

    def previous_row(y, c, zh, zl, x):
        r = y * sizes[1] + c
        zh = zh if r > 0 else (zh + 1) % sizes[2]
        r = (r - 1) % rows_count
        return r // sizes[1], r % sizes[1], zh, zl, x

    near = jnp.stack([near1, near2])
    gathered = lax.all_to_all(jnp.broadcast_to(near, (sizes[4],) + near.shape), "x", 0, 0)

    def partner(v, axis, n, j):
        return lax.ppermute(v, axis, [(i, i ^ j) for i in range(n)])

    wide = (sizes[4], WIN, slots, size // sizes[4], size)
    (parts,) = call(
        functools.partial(product_kernel, factor),
        1, [wide], [], WIN * slots * 6 * size**3,
        place, left, ahead, beside0, beside1, codes, home,
    )
    parts, gathered = lax.optimization_barrier((parts, gathered))
    next1 = lax.ppermute(gathered[:, 0], AXES, pairs_of(sizes, previous_row))
    (pack,) = call(
        pack_kernel, 1, [(3, sizes[4] * part, size)], [pltpu.VMEM((size, size), jnp.int32)], 10**6,
        place, codes, gathered, next1,
    )
    packs = [pack] + [partner(pack, "zl", sizes[3], j) for j in range(1, sizes[3])]
    parts = lax.all_to_all(parts, "x", 0, 0)
    parts, _ = lax.optimization_barrier((parts, pack))
    (ready,) = call(add_kernel, 0, [(slots * sizes[3], WIN, part, size)], [], 10**6, parts)
    ready, *packs = lax.optimization_barrier((ready, *packs))
    got = lax.all_to_all(ready, ("zh", "zl"), 0, 0)
    piece = part // slots
    sent = call(
        functools.partial(finish_kernel, factor),
        1, [(WIN, piece, size)] * 2, [pltpu.VMEM((3, size, size), F32), pltpu.VMEM((WIN, part, size), F32)],
        3 * 6 * part * size**2, place, got, *packs,
    )

    def sent_to(flip):
        def target(y, c, zh, zl, x):
            r = (y * sizes[1] + c - 2) % rows_count
            pick = zh if flip == 0 else 1 - zh
            n = 2 * (x * sizes[3] + zl) + pick
            return r // sizes[1], r % sizes[1], n // (sizes[3] * sizes[4]), n // sizes[4] % sizes[3], n % sizes[4]
        return target

    back = [lax.ppermute(sent[flip], AXES, pairs_of(sizes, sent_to(flip))) for flip in range(2)]
    (result,) = call(order_kernel, 1, [(WIN, slots, piece, size)], [], 10**4, place, *back)
    return result[:, :, None]


def solution(mesh):
    sizes = (mesh.shape["row"] // 2, 2, 2, mesh.shape["col"] // 8, 4)
    fine = Mesh(mesh.devices.reshape(sizes), AXES)
    rows, cols = AXES[:2], AXES[2:]
    placed = (P(None, rows, None, cols, None, None), P(None, rows, None, cols, None, None), P())
    return jax.shard_map(
        lambda *args: on_device(sizes, *args),
        mesh=fine,
        in_specs=placed,
        out_specs=P(None, None, rows, cols, None),
        check_vma=False,
    )
```

```python
import functools
import math

import jax
import jax.numpy as jnp
import numpy as np
from jax import lax
from jax.experimental import pallas as pl
from jax.experimental.pallas import tpu as pltpu
from jax.sharding import Mesh, PartitionSpec as P

TOP = 4
WIN = 3
AXES = ("y", "core", "zh", "zl", "x")
F32 = jnp.float32


def pairs_of(sizes, target):
    pairs = []
    for number in range(math.prod(sizes)):
        there = target(*(int(i) for i in np.unravel_index(number, sizes)))
        if there is not None:
            pairs.append((number, int(np.ravel_multi_index(there, sizes))))
    return pairs


def halves(x):
    high = x.astype(jnp.bfloat16)
    return high, (x - high.astype(F32)).astype(jnp.bfloat16)


def times(a, b):
    dims = (((1,), (1,)), ((), ()))
    dot = functools.partial(lax.dot_general, dimension_numbers=dims, preferred_element_type=F32)
    return dot(a[0], b[0]) + (dot(a[0], b[1]) + dot(a[1], b[0]))


def codes_of(codes, tile):
    return codes[pl.ds(jnp.clip(tile, 0, codes.shape[0] - 1), 1), :]


def partners_of(code):
    return jnp.where(code == 0, 8, jnp.where(code == 1, 4, jnp.where(code == 2, 10, 5)))


def columns_of(codes, tiles):
    total = partners_of(codes_of(codes, tiles[0]))
    for k, tile in enumerate(tiles[1:], 1):
        total = total + (partners_of(codes_of(codes, tile)) << (4 * k))
    size = codes.shape[1]
    return jnp.broadcast_to(total, (size, size)).T


def product_kernel(factor, place, left_ref, ahead_ref, beside0_ref, beside1_ref, codes, home_ref, out):
    row, col, core = place[0], place[1], place[3]
    slots, size = left_ref.shape[0], left_ref.shape[1]
    rows_count = codes.shape[0] // slots
    block = size // out.shape[0]
    col_bits = 1 << codes_of(codes, col)
    tile_rows = [slot * rows_count + row - 2 for slot in range(slots)]
    keys = [(slot, e) for e in (4, 3, 2) for slot in range(slots)]
    columns = columns_of(codes, [tile_rows[slot] + e for slot, e in keys])
    gap = lax.broadcasted_iota(jnp.int32, (size, size), 1) - lax.broadcasted_iota(jnp.int32, (size, size), 0)
    lefts = [left_ref[jnp.where(row < 2, 0, slot)] for slot in range(slots)]
    left_halves = [halves(left) for left in lefts]
    for k, (slot, e) in enumerate(keys):
        tile_row = tile_rows[slot]
        other = slots - 1 - slot
        allowed = (columns & (col_bits << (4 * k))) != 0
        if e == 4:
            tile = ahead_ref[jnp.where(row >= rows_count - 2, other, slot)]
            allowed = allowed & (gap > 3 - (col - tile_row - e) * size)
        elif e == 3:
            after = beside1_ref[jnp.where(row >= rows_count - 1, other, slot)]
            tile = jnp.where(core == 0, beside0_ref[slot], after)
        else:
            tile = home_ref[slot]
        right = halves(jnp.where(allowed, tile, 0.0))
        live = (tile_row >= 0) & (col > tile_row + TOP)
        scale = jnp.where(live, factor, 0.0).astype(F32)
        own = jnp.where((tile_row >= 0) & (col == tile_row + e), 1.0, 0.0).astype(F32)
        full = scale * times(left_halves[slot], right) + own * lefts[slot]
        for x in range(out.shape[0]):
            out[x, TOP - e, slot] = full[x * block:(x + 1) * block]


def add_kernel(got, out):
    slots, rows = got.shape[2:4]
    deep = out.shape[0] // slots
    piece = rows // deep
    for number in range(WIN):
        for slot in range(slots):
            total = got[0, number, slot]
            for k in range(1, got.shape[0]):
                total = total + got[k, number, slot]
            for z in range(deep):
                out[slot * deep + z, number] = total[z * piece:(z + 1) * piece]


def pack_kernel(wide, place, codes, gathered, next1, out, columns):
    row, half, x = place[0], place[2], place[4]
    count, part, size = gathered.shape[0], gathered.shape[2], out.shape[3]
    first = row + half * (codes.shape[0] // 2)
    columns[...] = columns_of(codes, [first, first + 1])
    steps = lax.broadcasted_iota(jnp.int32, (part, size), 1) - lax.broadcasted_iota(jnp.int32, (part, size), 0)
    for i in range(count):
        start = pl.multiple_of((i * wide + x) * part, part)
        down = columns[pl.ds(start, part), :]
        for k, (at, beyond) in enumerate(((0, 1), (0, 2), (1, 1))):
            piece = gathered[i, k] if k < 2 else next1[i]
            allowed = (down & (1 << (codes_of(codes, first + at + beyond) + 4 * at))) != 0
            far = steps > 3 + start - beyond * size
            out[k, i] = jnp.where(allowed & far, piece, 0.0)


def assemble_kernel(place, *refs):
    packs, high, low, whole = refs[:-3], refs[-3], refs[-2], refs[-1]
    x = place[4]
    _, deep, part, _ = packs[0].shape
    for k in range(3):
        for j, pack in enumerate(packs):
            for i in range(deep):
                start = pl.multiple_of((i * len(packs) + (x ^ j)) * part, part)
                whole[k, pl.ds(start, part), :] = pack[k, i]
        high[k], low[k] = halves(whole[k])


def finish_kernel(factor, place, got, high, low, out_a, out_b, rows):
    half = place[2]
    sums = []
    for w in range(WIN):
        total = got[0, w]
        for k in range(1, got.shape[0]):
            total = total + got[k, w]
        sums.append(total)
    w4 = sums[0]
    w4_halves = halves(w4)
    w3 = sums[1] + factor * times(w4_halves, (high[2], low[2]))
    w2 = sums[2] + factor * (times(w4_halves, (high[1], low[1])) + times(halves(w3), (high[0], low[0])))
    piece = out_a.shape[1]
    for w, value in enumerate((w4, w3, w2)):
        rows[w] = value
        out_a[w] = rows[w, pl.ds(pl.multiple_of(half * piece, piece), piece), :]
        out_b[w] = rows[w, pl.ds(pl.multiple_of((1 - half) * piece, piece), piece), :]


def order_kernel(place, back0, back1, out):
    swap = (place[1] + place[6]) % 2 == 1
    out[:, 0] = jnp.where(swap, back1[...], back0[...])
    out[:, 1] = jnp.where(swap, back0[...], back1[...])


def call(kernel, in_count, outs, scratch, flops, *args, kind=F32):
    spec = pl.BlockSpec(memory_space=pltpu.VMEM)
    moved = sum(math.prod(a.shape) * 4 for a in args) + sum(math.prod(s) * 4 for s in outs)
    return pl.pallas_call(
        kernel,
        out_shape=[jax.ShapeDtypeStruct(s, kind) for s in outs],
        in_specs=[pl.BlockSpec(memory_space=pltpu.SMEM)] * in_count + [spec] * (len(args) - in_count),
        out_specs=[spec] * len(outs),
        scratch_shapes=scratch,
        cost_estimate=pl.CostEstimate(flops=flops, bytes_accessed=moved, transcendentals=0),
        compiler_params=pltpu.CompilerParams(vmem_limit_bytes=24 * 1024 * 1024),
    )(*args)


def on_device(sizes, inside, outer, sequence):
    rows_count = sizes[0] * sizes[1]
    cols_count = sizes[2] * sizes[3] * sizes[4]
    size = inside.shape[-1]
    slots = inside.shape[0]
    tile_count = slots * rows_count
    part = slots * size // cols_count
    factor = 1.0 / math.sqrt(tile_count)
    core = lax.axis_index("core")
    row = lax.axis_index("y") * sizes[1] + core
    half = lax.axis_index("zh")
    col = lax.axis_index(AXES[2:])
    late = (row >= rows_count - 2).astype(jnp.int32)
    place = jnp.stack([row, col, half, core, lax.axis_index("x"), lax.axis_index("zl"), late]).astype(jnp.int32)
    home = inside[:, 0, 0, 0]
    out_tiles = outer[:, 0, 0, 0]

    def row_shift(v, by):
        n = sizes[0]
        return lax.ppermute(v, "y", [(i, (i + by) % n) for i in range(n)])

    left = row_shift(out_tiles, 1)
    ahead = row_shift(home, -1)
    beside0 = lax.ppermute(home, "core", [(1, 0)])
    left, ahead = lax.optimization_barrier((left, ahead))
    beside1 = lax.ppermute(ahead, "core", [(0, 1)])

    codes = sequence.reshape(tile_count, size)

    spread = lax.all_to_all(home.reshape(cols_count, part, size), AXES[2:], 0, 0)
    first = jnp.minimum(row + half * rows_count + 1, cols_count - 1)
    second = jnp.minimum(row + half * rows_count + 2, cols_count - 1)
    near1 = lax.dynamic_index_in_dim(spread, first, 0, False)
    near2 = lax.dynamic_index_in_dim(spread, second, 0, False)

    def previous_row(y, c, zh, zl, x):
        r = y * sizes[1] + c
        zh = zh if r > 0 else (zh + 1) % sizes[2]
        r = (r - 1) % rows_count
        return r // sizes[1], r % sizes[1], zh, zl, x

    near = jnp.stack([near1, near2])
    gathered = lax.all_to_all(jnp.broadcast_to(near, (sizes[3],) + near.shape), "zl", 0, 0)

    def partner(v, axis, n, j):
        return lax.ppermute(v, axis, [(i, i ^ j) for i in range(n)])

    wide = (sizes[4], WIN, slots, size // sizes[4], size)
    (parts,) = call(
        functools.partial(product_kernel, factor),
        1, [wide], [], WIN * slots * 6 * size**3,
        place, left, ahead, beside0, beside1, codes, home,
    )
    parts, gathered = lax.optimization_barrier((parts, gathered))
    next1 = lax.ppermute(gathered[:, 0], AXES, pairs_of(sizes, previous_row))
    (pack,) = call(
        functools.partial(pack_kernel, sizes[4]),
        1, [(3, sizes[3], part, size)], [pltpu.VMEM((size, size), jnp.int32)], 10**6,
        place, codes, gathered, next1,
    )
    packs = {j: partner(pack, "x", sizes[4], j) for j in (2, 1, 3)}
    high, low = call(
        assemble_kernel, 1, [(3, size, size)] * 2, [pltpu.VMEM((3, size, size), F32)], 2 * 10**10,
        place, pack, *(packs[j] for j in range(1, sizes[4])), kind=jnp.bfloat16,
    )
    parts = lax.all_to_all(parts, "x", 0, 0)
    parts, _ = lax.optimization_barrier((parts, pack))
    (ready,) = call(add_kernel, 0, [(slots * sizes[3], WIN, part, size)], [], 10**6, parts)
    got = lax.all_to_all(ready, ("zh", "zl"), 0, 0)
    piece = part // slots
    sent = call(
        functools.partial(finish_kernel, factor),
        1, [(WIN, piece, size)] * 2, [pltpu.VMEM((WIN, part, size), F32)],
        3 * 6 * part * size**2, place, got, high, low,
    )

    def sent_to(flip):
        def target(y, c, zh, zl, x):
            r = (y * sizes[1] + c - 2) % rows_count
            pick = zh if flip == 0 else 1 - zh
            n = 2 * (x * sizes[3] + zl) + pick
            return r // sizes[1], r % sizes[1], n // (sizes[3] * sizes[4]), n // sizes[4] % sizes[3], n % sizes[4]
        return target

    back = [lax.ppermute(sent[flip], AXES, pairs_of(sizes, sent_to(flip))) for flip in range(2)]
    (result,) = call(order_kernel, 1, [(WIN, slots, piece, size)], [], 10**4, place, *back)
    return result[:, :, None]


def solution(mesh):
    sizes = (mesh.shape["row"] // 2, 2, 2, mesh.shape["col"] // 8, 4)
    fine = Mesh(mesh.devices.reshape(sizes), AXES)
    rows, cols = AXES[:2], AXES[2:]
    placed = (P(None, rows, None, cols, None, None), P(None, rows, None, cols, None, None), P())
    return jax.shard_map(
        lambda *args: on_device(sizes, *args),
        mesh=fine,
        in_specs=placed,
        out_specs=P(None, None, rows, cols, None),
        check_vma=False,
    )
```

```python
import functools
import math

import jax
import jax.numpy as jnp
import numpy as np
from jax import lax
from jax.experimental import pallas as pl
from jax.experimental.pallas import tpu as pltpu
from jax.sharding import Mesh, PartitionSpec as P

TOP = 4
WIN = 3
AXES = ("y", "core", "zh", "zl", "x")
F32 = jnp.float32


def pairs_of(sizes, target):
    pairs = []
    for number in range(math.prod(sizes)):
        there = target(*(int(i) for i in np.unravel_index(number, sizes)))
        if there is not None:
            pairs.append((number, int(np.ravel_multi_index(there, sizes))))
    return pairs


def halves(x):
    high = x.astype(jnp.bfloat16)
    return high, (x - high.astype(F32)).astype(jnp.bfloat16)


def times(a, b):
    dims = (((1,), (1,)), ((), ()))
    dot = functools.partial(lax.dot_general, dimension_numbers=dims, preferred_element_type=F32)
    return dot(a[0], b[0]) + (dot(a[0], b[1]) + dot(a[1], b[0]))


def codes_of(codes, tile):
    return codes[pl.ds(jnp.clip(tile, 0, codes.shape[0] - 1), 1), :]


def partners_of(code):
    return jnp.where(code == 0, 8, jnp.where(code == 1, 4, jnp.where(code == 2, 10, 5)))


def columns_of(codes, tiles):
    total = partners_of(codes_of(codes, tiles[0]))
    for k, tile in enumerate(tiles[1:], 1):
        total = total + (partners_of(codes_of(codes, tile)) << (4 * k))
    size = codes.shape[1]
    return jnp.broadcast_to(total, (size, size)).T


def product_kernel(factor, place, left_ref, ahead_ref, beside_ref, codes, home_ref, out):
    row, col = place[0], place[1]
    slots, size = left_ref.shape[0], left_ref.shape[1]
    rows_count = codes.shape[0] // slots
    block = size // out.shape[0]
    col_bits = 1 << codes_of(codes, col)
    tile_rows = [slot * rows_count + row - 2 for slot in range(slots)]
    keys = [(slot, e) for e in (4, 3, 2) for slot in range(slots)]
    columns = columns_of(codes, [tile_rows[slot] + e for slot, e in keys])
    gap = lax.broadcasted_iota(jnp.int32, (size, size), 1) - lax.broadcasted_iota(jnp.int32, (size, size), 0)
    lefts = [left_ref[jnp.where(row < 2, 0, slot)] for slot in range(slots)]
    left_halves = [halves(left) for left in lefts]
    for k, (slot, e) in enumerate(keys):
        tile_row = tile_rows[slot]
        other = slots - 1 - slot
        allowed = (columns & (col_bits << (4 * k))) != 0
        if e == 4:
            tile = ahead_ref[jnp.where(row >= rows_count - 2, other, slot)]
            allowed = allowed & (gap > 3 - (col - tile_row - e) * size)
        elif e == 3:
            tile = beside_ref[jnp.where(row >= rows_count - 1, other, slot)]
        else:
            tile = home_ref[slot]
        right = halves(jnp.where(allowed, tile, 0.0))
        live = (tile_row >= 0) & (col > tile_row + TOP)
        scale = jnp.where(live, factor, 0.0).astype(F32)
        own = jnp.where((tile_row >= 0) & (col == tile_row + e), 1.0, 0.0).astype(F32)
        full = scale * times(left_halves[slot], right) + own * lefts[slot]
        for x in range(out.shape[0]):
            out[x, TOP - e, slot] = full[x * block:(x + 1) * block]


def add_kernel(got, out):
    slots, rows = got.shape[2:4]
    deep = out.shape[0] // slots
    piece = rows // deep
    for number in range(WIN):
        for slot in range(slots):
            total = got[0, number, slot]
            for k in range(1, got.shape[0]):
                total = total + got[k, number, slot]
            for z in range(deep):
                out[slot * deep + z, number] = total[z * piece:(z + 1) * piece]


def pack_kernel(wide, place, codes, gathered, next1, out, columns):
    row, half, x = place[0], place[2], place[4]
    count, part, size = gathered.shape[0], gathered.shape[2], out.shape[3]
    first = row + half * (codes.shape[0] // 2)
    columns[...] = columns_of(codes, [first, first + 1])
    steps = lax.broadcasted_iota(jnp.int32, (part, size), 1) - lax.broadcasted_iota(jnp.int32, (part, size), 0)
    for i in range(count):
        start = pl.multiple_of((i * wide + x) * part, part)
        down = columns[pl.ds(start, part), :]
        for k, (at, beyond) in enumerate(((0, 1), (0, 2), (1, 1))):
            piece = gathered[i, k] if k < 2 else next1[i]
            allowed = (down & (1 << (codes_of(codes, first + at + beyond) + 4 * at))) != 0
            far = steps > 3 + start - beyond * size
            out[k, i] = jnp.where(allowed & far, piece, 0.0)


def assemble_kernel(order, place, *refs):
    packs, high, low, whole = refs[:-3], refs[-3], refs[-2], refs[-1]
    x = place[4]
    _, deep, part, _ = packs[0].shape
    for k in range(3):
        for j, pack in zip(order, packs):
            for i in range(deep):
                start = pl.multiple_of((i * len(packs) + (x ^ j)) * part, part)
                whole[k, pl.ds(start, part), :] = pack[k, i]
        high[k], low[k] = halves(whole[k])


def finish_kernel(factor, place, got, high, low, out_a, out_b, rows):
    half = place[2]
    sums = []
    for w in range(WIN):
        total = got[0, w]
        for k in range(1, got.shape[0]):
            total = total + got[k, w]
        sums.append(total)
    w4 = sums[0]
    w4_halves = halves(w4)
    w3 = sums[1] + factor * times(w4_halves, (high[2], low[2]))
    w2 = sums[2] + factor * (times(w4_halves, (high[1], low[1])) + times(halves(w3), (high[0], low[0])))
    piece = out_a.shape[1]
    for w, value in enumerate((w4, w3, w2)):
        rows[w] = value
        out_a[w] = rows[w, pl.ds(pl.multiple_of(half * piece, piece), piece), :]
        out_b[w] = rows[w, pl.ds(pl.multiple_of((1 - half) * piece, piece), piece), :]


def order_kernel(place, back0, back1, out):
    swap = (place[1] + place[6]) % 2 == 1
    out[:, 0] = jnp.where(swap, back1[...], back0[...])
    out[:, 1] = jnp.where(swap, back0[...], back1[...])


def call(kernel, in_count, outs, scratch, flops, *args, kind=F32):
    spec = pl.BlockSpec(memory_space=pltpu.VMEM)
    moved = sum(math.prod(a.shape) * 4 for a in args) + sum(math.prod(s) * 4 for s in outs)
    return pl.pallas_call(
        kernel,
        out_shape=[jax.ShapeDtypeStruct(s, kind) for s in outs],
        in_specs=[pl.BlockSpec(memory_space=pltpu.SMEM)] * in_count + [spec] * (len(args) - in_count),
        out_specs=[spec] * len(outs),
        scratch_shapes=scratch,
        cost_estimate=pl.CostEstimate(flops=flops, bytes_accessed=moved, transcendentals=0),
        compiler_params=pltpu.CompilerParams(vmem_limit_bytes=24 * 1024 * 1024),
    )(*args)


def on_device(sizes, inside, outer, sequence):
    rows_count = sizes[0] * sizes[1]
    cols_count = sizes[2] * sizes[3] * sizes[4]
    size = inside.shape[-1]
    slots = inside.shape[0]
    tile_count = slots * rows_count
    part = slots * size // cols_count
    factor = 1.0 / math.sqrt(tile_count)
    core = lax.axis_index("core")
    row = lax.axis_index("y") * sizes[1] + core
    half = lax.axis_index("zh")
    col = lax.axis_index(AXES[2:])
    late = (row >= rows_count - 2).astype(jnp.int32)
    place = jnp.stack([row, col, half, core, lax.axis_index("x"), lax.axis_index("zl"), late]).astype(jnp.int32)
    home = inside[:, 0, 0, 0]
    out_tiles = outer[:, 0, 0, 0]

    def row_shift(v, by):
        n = sizes[0]
        return lax.ppermute(v, "y", [(i, (i + by) % n) for i in range(n)])

    left = row_shift(out_tiles, 1)
    beside = lax.ppermute(home, AXES[:2], [(i, (i - 1) % rows_count) for i in range(rows_count)])
    ahead = row_shift(home, -1)

    codes = sequence.reshape(tile_count, size)

    spread = lax.all_to_all(home.reshape(cols_count, part, size), AXES[2:], 0, 0)
    first = jnp.minimum(row + half * rows_count + 1, cols_count - 1)
    second = jnp.minimum(row + half * rows_count + 2, cols_count - 1)
    near1 = lax.dynamic_index_in_dim(spread, first, 0, False)
    near2 = lax.dynamic_index_in_dim(spread, second, 0, False)

    def previous_row(y, c, zh, zl, x):
        r = y * sizes[1] + c
        zh = zh if r > 0 else (zh + 1) % sizes[2]
        r = (r - 1) % rows_count
        return r // sizes[1], r % sizes[1], zh, zl, x

    near = jnp.stack([near1, near2])
    gathered = lax.all_to_all(jnp.broadcast_to(near, (sizes[3],) + near.shape), "zl", 0, 0)

    def partner(v, axis, n, j):
        return lax.ppermute(v, axis, [(i, i ^ j) for i in range(n)])

    wide = (sizes[4], WIN, slots, size // sizes[4], size)
    (parts,) = call(
        functools.partial(product_kernel, factor),
        1, [wide], [], WIN * slots * 6 * size**3,
        place, left, ahead, beside, codes, home,
    )
    parts, gathered = lax.optimization_barrier((parts, gathered))
    next1 = lax.ppermute(gathered[:, 0], AXES, pairs_of(sizes, previous_row))
    (pack,) = call(
        functools.partial(pack_kernel, sizes[4]),
        1, [(3, sizes[3], part, size)], [pltpu.VMEM((size, size), jnp.int32)], 10**6,
        place, codes, gathered, next1,
    )
    order = (0, 1, 3, 2)
    packs = [pack] + [partner(pack, "x", sizes[4], j) for j in order[1:]]
    high, low = call(
        functools.partial(assemble_kernel, order), 1, [(3, size, size)] * 2, [pltpu.VMEM((3, size, size), F32)], 2 * 10**10,
        place, *packs, kind=jnp.bfloat16,
    )
    parts = lax.all_to_all(parts, "x", 0, 0)
    parts, _ = lax.optimization_barrier((parts, pack))
    (ready,) = call(add_kernel, 0, [(slots * sizes[3], WIN, part, size)], [], 10**6, parts)
    got = lax.all_to_all(ready, ("zh", "zl"), 0, 0)
    piece = part // slots
    sent = call(
        functools.partial(finish_kernel, factor),
        1, [(WIN, piece, size)] * 2, [pltpu.VMEM((WIN, part, size), F32)],
        3 * 6 * part * size**2, place, got, high, low,
    )

    def sent_to(flip):
        def target(y, c, zh, zl, x):
            r = (y * sizes[1] + c - 2) % rows_count
            pick = zh if flip == 0 else 1 - zh
            n = 2 * (x * sizes[3] + zl) + pick
            return r // sizes[1], r % sizes[1], n // (sizes[3] * sizes[4]), n // sizes[4] % sizes[3], n % sizes[4]
        return target

    back = [lax.ppermute(sent[flip], AXES, pairs_of(sizes, sent_to(flip))) for flip in range(2)]
    (result,) = call(order_kernel, 1, [(WIN, slots, piece, size)], [], 10**4, place, *back)
    return result[:, :, None]


def solution(mesh):
    sizes = (mesh.shape["row"] // 2, 2, 2, mesh.shape["col"] // 8, 4)
    fine = Mesh(mesh.devices.reshape(sizes), AXES)
    rows, cols = AXES[:2], AXES[2:]
    placed = (P(None, rows, None, cols, None, None), P(None, rows, None, cols, None, None), P())
    return jax.shard_map(
        lambda *args: on_device(sizes, *args),
        mesh=fine,
        in_specs=placed,
        out_specs=P(None, None, rows, cols, None),
        check_vma=False,
    )
```

```python
import functools
import math

import jax
import jax.numpy as jnp
import numpy as np
from jax import lax
from jax.experimental import pallas as pl
from jax.experimental.pallas import tpu as pltpu
from jax.sharding import Mesh, PartitionSpec as P

TOP = 4
WIN = 3
AXES = ("y", "core", "zh", "zl", "x")
F32 = jnp.float32


def pairs_of(sizes, target):
    pairs = []
    for number in range(math.prod(sizes)):
        there = target(*(int(i) for i in np.unravel_index(number, sizes)))
        if there is not None:
            pairs.append((number, int(np.ravel_multi_index(there, sizes))))
    return pairs


def halves(x):
    high = x.astype(jnp.bfloat16)
    return high, (x - high.astype(F32)).astype(jnp.bfloat16)


def times(a, b):
    dims = (((1,), (1,)), ((), ()))
    dot = functools.partial(lax.dot_general, dimension_numbers=dims, preferred_element_type=F32)
    return dot(a[0], b[0]) + (dot(a[0], b[1]) + dot(a[1], b[0]))


def codes_of(codes, tile):
    return codes[pl.ds(jnp.clip(tile, 0, codes.shape[0] - 1), 1), :]


def partners_of(code):
    return jnp.where(code == 0, 8, jnp.where(code == 1, 4, jnp.where(code == 2, 10, 5)))


def columns_of(codes, tiles):
    total = partners_of(codes_of(codes, tiles[0]))
    for k, tile in enumerate(tiles[1:], 1):
        total = total + (partners_of(codes_of(codes, tile)) << (4 * k))
    size = codes.shape[1]
    return jnp.broadcast_to(total, (size, size)).T


def columns_kernel(slots, place, codes, for_products, for_pack):
    row, half = place[0], place[2]
    rows_count = codes.shape[0] // slots
    for_products[...] = columns_of(codes, [slot * rows_count + row - 2 + e for e in (4, 3, 2) for slot in range(slots)])
    first = row + half * rows_count
    for_pack[...] = columns_of(codes, [first, first + 1])


def product_kernel(factor, place, left_ref, ahead_ref, beside_ref, codes, columns_ref, home_ref, out):
    row, col = place[0], place[1]
    slots, size = left_ref.shape[0], left_ref.shape[1]
    rows_count = codes.shape[0] // slots
    piece = size // codes.shape[0]
    chunks = size // out.shape[0] // piece
    col_bits = 1 << codes_of(codes, col)
    tile_rows = [slot * rows_count + row - 2 for slot in range(slots)]
    keys = [(slot, e) for e in (4, 3, 2) for slot in range(slots)]
    columns = columns_ref[...]
    gap = lax.broadcasted_iota(jnp.int32, (size, size), 1) - lax.broadcasted_iota(jnp.int32, (size, size), 0)
    lefts = [left_ref[jnp.where(row < 2, 0, slot)] for slot in range(slots)]
    left_halves = [halves(left) for left in lefts]
    for k, (slot, e) in enumerate(keys):
        tile_row = tile_rows[slot]
        other = slots - 1 - slot
        allowed = (columns & (col_bits << (4 * k))) != 0
        if e == 4:
            tile = ahead_ref[jnp.where(row >= rows_count - 2, other, slot)]
            allowed = allowed & (gap > 3 - (col - tile_row - e) * size)
        elif e == 3:
            tile = beside_ref[jnp.where(row >= rows_count - 1, other, slot)]
        else:
            tile = home_ref[slot]
        right = halves(jnp.where(allowed, tile, 0.0))
        live = (tile_row >= 0) & (col > tile_row + TOP)
        scale = jnp.where(live, factor, 0.0).astype(F32)
        own = jnp.where((tile_row >= 0) & (col == tile_row + e), 1.0, 0.0).astype(F32)
        full = scale * times(left_halves[slot], right) + own * lefts[slot]
        for x in range(out.shape[0]):
            for chunk in range(chunks):
                start = (chunk % slots) * (size // slots) + (chunk // slots * out.shape[0] + x) * piece
                out[x, TOP - e, slot, chunk * piece:(chunk + 1) * piece] = full[start:start + piece]


def add_kernel(got, out):
    slots, rows = got.shape[2:4]
    deep = out.shape[0] // slots
    piece = rows // deep
    for number in range(WIN):
        for slot in range(slots):
            total = got[0, number, slot]
            for k in range(1, got.shape[0]):
                total = total + got[k, number, slot]
            for z in range(deep):
                out[slot * deep + z, number] = total[z * piece:(z + 1) * piece]


def pack_kernel(wide, place, codes, columns, gathered, next1, out):
    row, half, x = place[0], place[2], place[4]
    count, part, size = gathered.shape[0], gathered.shape[2], out.shape[3]
    first = row + half * (codes.shape[0] // 2)
    steps = lax.broadcasted_iota(jnp.int32, (part, size), 1) - lax.broadcasted_iota(jnp.int32, (part, size), 0)
    for i in range(count):
        start = pl.multiple_of((i * wide + x) * part, part)
        down = columns[pl.ds(start, part), :]
        for k, (at, beyond) in enumerate(((0, 1), (0, 2), (1, 1))):
            piece = gathered[i, k] if k < 2 else next1[i]
            allowed = (down & (1 << (codes_of(codes, first + at + beyond) + 4 * at))) != 0
            far = steps > 3 + start - beyond * size
            out[k, i] = jnp.where(allowed & far, piece, 0.0)


def assemble_kernel(order, place, *refs):
    packs, high, low, whole = refs[:-3], refs[-3], refs[-2], refs[-1]
    x = place[4]
    _, deep, part, _ = packs[0].shape
    for k in range(3):
        for j, pack in zip(order, packs):
            for i in range(deep):
                start = pl.multiple_of((i * len(packs) + (x ^ j)) * part, part)
                whole[k, pl.ds(start, part), :] = pack[k, i]
        high[k], low[k] = halves(whole[k])


def finish_kernel(factor, place, got, high, low, out_a, out_b, rows):
    half = place[2]
    sums = []
    for w in range(WIN):
        total = got[0, w]
        for k in range(1, got.shape[0]):
            total = total + got[k, w]
        sums.append(total)
    w4 = sums[0]
    w4_halves = halves(w4)
    w3 = sums[1] + factor * times(w4_halves, (high[2], low[2]))
    w2 = sums[2] + factor * (times(w4_halves, (high[1], low[1])) + times(halves(w3), (high[0], low[0])))
    piece = out_a.shape[1]
    for w, value in enumerate((w4, w3, w2)):
        rows[w] = value
        out_a[w] = rows[w, pl.ds(pl.multiple_of(half * piece, piece), piece), :]
        out_b[w] = rows[w, pl.ds(pl.multiple_of((1 - half) * piece, piece), piece), :]


def order_kernel(place, back0, back1, out):
    swap = (place[2] + place[6]) % 2 == 1
    out[:, 0] = jnp.where(swap, back1[...], back0[...])
    out[:, 1] = jnp.where(swap, back0[...], back1[...])


def call(kernel, in_count, outs, scratch, flops, *args, kind=F32):
    spec = pl.BlockSpec(memory_space=pltpu.VMEM)
    moved = sum(math.prod(a.shape) * 4 for a in args) + sum(math.prod(s) * 4 for s in outs)
    return pl.pallas_call(
        kernel,
        out_shape=[jax.ShapeDtypeStruct(s, kind) for s in outs],
        in_specs=[pl.BlockSpec(memory_space=pltpu.SMEM)] * in_count + [spec] * (len(args) - in_count),
        out_specs=[spec] * len(outs),
        scratch_shapes=scratch,
        cost_estimate=pl.CostEstimate(flops=flops, bytes_accessed=moved, transcendentals=0),
        compiler_params=pltpu.CompilerParams(vmem_limit_bytes=24 * 1024 * 1024),
    )(*args)


def on_device(sizes, inside, outer, sequence):
    rows_count = sizes[0] * sizes[1]
    cols_count = sizes[2] * sizes[3] * sizes[4]
    size = inside.shape[-1]
    slots = inside.shape[0]
    tile_count = slots * rows_count
    part = slots * size // cols_count
    factor = 1.0 / math.sqrt(tile_count)
    core = lax.axis_index("core")
    row = lax.axis_index("y") * sizes[1] + core
    half = lax.axis_index("zh")
    col = lax.axis_index(AXES[2:])
    late = (row >= rows_count - 2).astype(jnp.int32)
    place = jnp.stack([row, col, half, core, lax.axis_index("x"), lax.axis_index("zl"), late]).astype(jnp.int32)
    home = inside[:, 0, 0, 0]
    out_tiles = outer[:, 0, 0, 0]

    def row_shift(v, by):
        n = sizes[0]
        return lax.ppermute(v, "y", [(i, (i + by) % n) for i in range(n)])

    left = row_shift(out_tiles, 1)
    beside = lax.ppermute(home, AXES[:2], [(i, (i - 1) % rows_count) for i in range(rows_count)])
    ahead = row_shift(home, -1)

    codes = sequence.reshape(tile_count, size)
    columns, pack_columns = call(
        functools.partial(columns_kernel, slots), 1, [(size, size)] * 2, [], 10**6, place, codes, kind=jnp.int32
    )

    spread = lax.all_to_all(home.reshape(cols_count, part, size), AXES[2:], 0, 0)
    spread, columns, pack_columns = lax.optimization_barrier((spread, columns, pack_columns))
    first = jnp.minimum(row + half * rows_count + 1, cols_count - 1)
    second = jnp.minimum(row + half * rows_count + 2, cols_count - 1)
    near1 = lax.dynamic_index_in_dim(spread, first, 0, False)
    near2 = lax.dynamic_index_in_dim(spread, second, 0, False)

    def previous_row(y, c, zh, zl, x):
        r = y * sizes[1] + c
        zh = zh if r > 0 else (zh + 1) % sizes[2]
        r = (r - 1) % rows_count
        return r // sizes[1], r % sizes[1], zh, zl, x

    near = jnp.stack([near1, near2])
    gathered = lax.all_to_all(jnp.broadcast_to(near, (sizes[3],) + near.shape), "zl", 0, 0)

    def partner(v, axis, n, j):
        return lax.ppermute(v, axis, [(i, i ^ j) for i in range(n)])

    wide = (sizes[4], WIN, slots, size // sizes[4], size)
    (parts,) = call(
        functools.partial(product_kernel, factor),
        1, [wide], [], WIN * slots * 6 * size**3,
        place, left, ahead, beside, codes, columns, home,
    )
    parts, gathered = lax.optimization_barrier((parts, gathered))
    next1 = lax.ppermute(gathered[:, 0], AXES, pairs_of(sizes, previous_row))
    (pack,) = call(
        functools.partial(pack_kernel, sizes[4]),
        1, [(3, sizes[3], part, size)], [], 10**6, place, codes, pack_columns, gathered, next1,
    )
    order = (0, 1, 3, 2)
    packs = [pack] + [partner(pack, "x", sizes[4], j) for j in order[1:]]
    high, low = call(
        functools.partial(assemble_kernel, order), 1, [(3, size, size)] * 2, [pltpu.VMEM((3, size, size), F32)], 2 * 10**10,
        place, *packs, kind=jnp.bfloat16,
    )
    parts = lax.all_to_all(parts, "x", 0, 0)
    parts, _ = lax.optimization_barrier((parts, pack))
    (ready,) = call(add_kernel, 0, [(slots * sizes[3], WIN, part, size)], [], 10**6, parts)
    got = lax.all_to_all(ready, ("zh", "zl"), 0, 0)
    piece = part // slots
    sent = call(
        functools.partial(finish_kernel, factor),
        1, [(WIN, piece, size)] * 2, [pltpu.VMEM((WIN, part, size), F32)],
        3 * 6 * part * size**2, place, got, high, low,
    )

    def sent_to(flip):
        def target(y, c, zh, zl, x):
            return (y - 1) % sizes[0], c, zh ^ flip, zl, x
        return target

    back = [lax.ppermute(sent[flip], AXES, pairs_of(sizes, sent_to(flip))) for flip in range(2)]
    (result,) = call(order_kernel, 1, [(WIN, slots, piece, size)], [], 10**4, place, *back)
    return result[:, :, None]


def solution(mesh):
    sizes = (mesh.shape["row"] // 2, 2, 2, mesh.shape["col"] // 8, 4)
    fine = Mesh(mesh.devices.reshape(sizes), AXES)
    rows, cols = AXES[:2], AXES[2:]
    placed = (P(None, rows, None, cols, None, None), P(None, rows, None, cols, None, None), P())
    return jax.shard_map(
        lambda *args: on_device(sizes, *args),
        mesh=fine,
        in_specs=placed,
        out_specs=P(None, None, rows, cols, None),
        check_vma=False,
    )
```

```python
import functools
import math

import jax
import jax.numpy as jnp
import numpy as np
from jax import lax
from jax.experimental import pallas as pl
from jax.experimental.pallas import tpu as pltpu
from jax.sharding import Mesh, PartitionSpec as P

TOP = 4
WIN = 3
AXES = ("y", "core", "zh", "zl", "x")
F32 = jnp.float32


def pairs_of(sizes, target):
    pairs = []
    for number in range(math.prod(sizes)):
        there = target(*(int(i) for i in np.unravel_index(number, sizes)))
        if there is not None:
            pairs.append((number, int(np.ravel_multi_index(there, sizes))))
    return pairs


def halves(x):
    high = x.astype(jnp.bfloat16)
    return high, (x - high.astype(F32)).astype(jnp.bfloat16)


def times(a, b):
    dims = (((1,), (1,)), ((), ()))
    dot = functools.partial(lax.dot_general, dimension_numbers=dims, preferred_element_type=F32)
    return dot(a[0], b[0]) + (dot(a[0], b[1]) + dot(a[1], b[0]))


def codes_of(codes, tile):
    return codes[pl.ds(jnp.clip(tile, 0, codes.shape[0] - 1), 1), :]


def partners_of(code):
    return jnp.where(code == 0, 8, jnp.where(code == 1, 4, jnp.where(code == 2, 10, 5)))


def columns_of(codes, tiles):
    total = partners_of(codes_of(codes, tiles[0]))
    for k, tile in enumerate(tiles[1:], 1):
        total = total + (partners_of(codes_of(codes, tile)) << (4 * k))
    size = codes.shape[1]
    return jnp.broadcast_to(total, (size, size)).T


def columns_kernel(slots, place, codes, for_products, for_pack):
    row, half = place[0], place[2]
    rows_count = codes.shape[0] // slots
    for_products[...] = columns_of(codes, [slot * rows_count + row - 2 + e for e in (4, 3, 2) for slot in range(slots)])
    first = row + half * rows_count
    for_pack[...] = columns_of(codes, [first, first + 1])


def product_kernel(factor, place, left_ref, ahead_ref, beside_ref, codes, columns_ref, home_ref, sent, out, sems):
    row, col = place[0], place[1]
    slots, size = left_ref.shape[0], left_ref.shape[1]
    rows_count = codes.shape[0] // slots
    piece = size // codes.shape[0]
    chunks = size // out.shape[0] // piece
    col_bits = 1 << codes_of(codes, col)
    tile_rows = [slot * rows_count + row - 2 for slot in range(slots)]
    keys = [(slot, e) for e in (4, 3, 2) for slot in range(slots)]
    columns = columns_ref[...]
    gap = lax.broadcasted_iota(jnp.int32, (size, size), 1) - lax.broadcasted_iota(jnp.int32, (size, size), 0)
    lefts = [left_ref[jnp.where(row < 2, 0, slot)] for slot in range(slots)]
    left_halves = [halves(left) for left in lefts]
    copies = []
    for k, (slot, e) in enumerate(keys):
        tile_row = tile_rows[slot]
        other = slots - 1 - slot
        allowed = (columns & (col_bits << (4 * k))) != 0
        if e == 4:
            tile = ahead_ref[jnp.where(row >= rows_count - 2, other, slot)]
            allowed = allowed & (gap > 3 - (col - tile_row - e) * size)
        elif e == 3:
            tile = beside_ref[jnp.where(row >= rows_count - 1, other, slot)]
        else:
            tile = home_ref[slot]
        right = halves(jnp.where(allowed, tile, 0.0))
        live = (tile_row >= 0) & (col > tile_row + TOP)
        scale = jnp.where(live, factor, 0.0).astype(F32)
        own = jnp.where((tile_row >= 0) & (col == tile_row + e), 1.0, 0.0).astype(F32)
        full = scale * times(left_halves[slot], right) + own * lefts[slot]
        for x in range(out.shape[0]):
            for chunk in range(chunks):
                start = (chunk % slots) * (size // slots) + (chunk // slots * out.shape[0] + x) * piece
                out[x, TOP - e, slot, chunk * piece:(chunk + 1) * piece] = full[start:start + piece]
        copies.append(pltpu.make_async_copy(out.at[:, TOP - e, slot], sent.at[:, TOP - e, slot], sems.at[k]))
        copies[-1].start()
    for copy in copies:
        copy.wait()


def add_kernel(got, out):
    slots, rows = got.shape[2:4]
    deep = out.shape[0] // slots
    piece = rows // deep
    for number in range(WIN):
        for slot in range(slots):
            total = got[0, number, slot]
            for k in range(1, got.shape[0]):
                total = total + got[k, number, slot]
            for z in range(deep):
                out[slot * deep + z, number] = total[z * piece:(z + 1) * piece]


def pack_kernel(wide, place, codes, columns, gathered, next1, out):
    row, half, x = place[0], place[2], place[4]
    count, part, size = gathered.shape[0], gathered.shape[2], out.shape[3]
    first = row + half * (codes.shape[0] // 2)
    steps = lax.broadcasted_iota(jnp.int32, (part, size), 1) - lax.broadcasted_iota(jnp.int32, (part, size), 0)
    for i in range(count):
        start = pl.multiple_of((i * wide + x) * part, part)
        down = columns[pl.ds(start, part), :]
        for k, (at, beyond) in enumerate(((0, 1), (0, 2), (1, 1))):
            piece = gathered[i, k] if k < 2 else next1[i]
            allowed = (down & (1 << (codes_of(codes, first + at + beyond) + 4 * at))) != 0
            far = steps > 3 + start - beyond * size
            out[k, i] = jnp.where(allowed & far, piece, 0.0)


def assemble_kernel(order, place, *refs):
    packs, high, low, whole = refs[:-3], refs[-3], refs[-2], refs[-1]
    x = place[4]
    _, deep, part, _ = packs[0].shape
    for k in range(3):
        for j, pack in zip(order, packs):
            for i in range(deep):
                start = pl.multiple_of((i * len(packs) + (x ^ j)) * part, part)
                whole[k, pl.ds(start, part), :] = pack[k, i]
        high[k], low[k] = halves(whole[k])


def finish_kernel(factor, place, got, high, low, out_a, out_b, rows):
    half = place[2]
    sums = []
    for w in range(WIN):
        total = got[0, w]
        for k in range(1, got.shape[0]):
            total = total + got[k, w]
        sums.append(total)
    w4 = sums[0]
    w4_halves = halves(w4)
    w3 = sums[1] + factor * times(w4_halves, (high[2], low[2]))
    w2 = sums[2] + factor * (times(w4_halves, (high[1], low[1])) + times(halves(w3), (high[0], low[0])))
    piece = out_a.shape[1]
    for w, value in enumerate((w4, w3, w2)):
        rows[w] = value
        out_a[w] = rows[w, pl.ds(pl.multiple_of(half * piece, piece), piece), :]
        out_b[w] = rows[w, pl.ds(pl.multiple_of((1 - half) * piece, piece), piece), :]


def order_kernel(place, back1, back0, out):
    swap = (place[2] + place[6]) % 2 == 1
    out[:, 0] = jnp.where(swap, back1[...], back0[...])
    out[:, 1] = jnp.where(swap, back0[...], back1[...])


def call(kernel, in_count, outs, scratch, flops, *args, kind=F32, space=pltpu.VMEM):
    spec = pl.BlockSpec(memory_space=pltpu.VMEM)
    moved = sum(math.prod(a.shape) * 4 for a in args) + sum(math.prod(s) * 4 for s in outs)
    return pl.pallas_call(
        kernel,
        out_shape=[jax.ShapeDtypeStruct(s, kind) for s in outs],
        in_specs=[pl.BlockSpec(memory_space=pltpu.SMEM)] * in_count + [spec] * (len(args) - in_count),
        out_specs=[pl.BlockSpec(memory_space=space)] * len(outs),
        scratch_shapes=scratch,
        cost_estimate=pl.CostEstimate(flops=flops, bytes_accessed=moved, transcendentals=0),
        compiler_params=pltpu.CompilerParams(vmem_limit_bytes=24 * 1024 * 1024),
    )(*args)


def on_device(sizes, inside, outer, sequence):
    rows_count = sizes[0] * sizes[1]
    cols_count = sizes[2] * sizes[3] * sizes[4]
    size = inside.shape[-1]
    slots = inside.shape[0]
    tile_count = slots * rows_count
    part = slots * size // cols_count
    factor = 1.0 / math.sqrt(tile_count)
    core = lax.axis_index("core")
    row = lax.axis_index("y") * sizes[1] + core
    half = lax.axis_index("zh")
    col = lax.axis_index(AXES[2:])
    late = (row >= rows_count - 2).astype(jnp.int32)
    place = jnp.stack([row, col, half, core, lax.axis_index("x"), lax.axis_index("zl"), late]).astype(jnp.int32)
    home = inside[:, 0, 0, 0]
    out_tiles = outer[:, 0, 0, 0]

    def row_shift(v, by):
        n = sizes[0]
        return lax.ppermute(v, "y", [(i, (i + by) % n) for i in range(n)])

    left = row_shift(out_tiles, 1)
    beside = lax.ppermute(home, AXES[:2], [(i, (i - 1) % rows_count) for i in range(rows_count)])
    ahead = row_shift(home, -1)

    codes = sequence.reshape(tile_count, size)
    columns, pack_columns = call(
        functools.partial(columns_kernel, slots), 1, [(size, size)] * 2, [], 10**6, place, codes, kind=jnp.int32
    )

    spread = lax.all_to_all(home.reshape(cols_count, part, size), AXES[2:], 0, 0)
    spread, columns, pack_columns = lax.optimization_barrier((spread, columns, pack_columns))
    first = jnp.minimum(row + half * rows_count + 1, cols_count - 1)
    second = jnp.minimum(row + half * rows_count + 2, cols_count - 1)
    near1 = lax.dynamic_index_in_dim(spread, first, 0, False)
    near2 = lax.dynamic_index_in_dim(spread, second, 0, False)

    def previous_row(y, c, zh, zl, x):
        r = y * sizes[1] + c
        zh = zh if r > 0 else (zh + 1) % sizes[2]
        r = (r - 1) % rows_count
        return r // sizes[1], r % sizes[1], zh, zl, x

    near = jnp.stack([near1, near2])
    gathered = lax.all_to_all(jnp.broadcast_to(near, (sizes[3],) + near.shape), "zl", 0, 0)

    def partner(v, axis, n, j):
        return lax.ppermute(v, axis, [(i, i ^ j) for i in range(n)])

    wide = (sizes[4], WIN, slots, size // sizes[4], size)
    (parts,) = call(
        functools.partial(product_kernel, factor),
        1, [wide], [pltpu.VMEM(wide, F32), pltpu.SemaphoreType.DMA((WIN * slots,))], WIN * slots * 6 * size**3,
        place, left, ahead, beside, codes, columns, home, space=pl.ANY,
    )
    parts, gathered = lax.optimization_barrier((parts, gathered))
    next1 = lax.ppermute(gathered[:, 0], AXES, pairs_of(sizes, previous_row))
    (pack,) = call(
        functools.partial(pack_kernel, sizes[4]),
        1, [(3, sizes[3], part, size)], [], 10**6, place, codes, pack_columns, gathered, next1,
    )
    order = (0, 1, 3, 2)
    packs = [pack] + [partner(pack, "x", sizes[4], j) for j in order[1:]]
    high, low = call(
        functools.partial(assemble_kernel, order), 1, [(3, size, size)] * 2, [pltpu.VMEM((3, size, size), F32)], 2 * 10**10,
        place, *packs, kind=jnp.bfloat16,
    )
    parts = lax.all_to_all(parts, "x", 0, 0)
    parts, _ = lax.optimization_barrier((parts, pack))
    (ready,) = call(add_kernel, 0, [(slots * sizes[3], WIN, part, size)], [], 10**6, parts)
    got = lax.all_to_all(ready, ("zh", "zl"), 0, 0)
    piece = part // slots
    sent = call(
        functools.partial(finish_kernel, factor),
        1, [(WIN, piece, size)] * 2, [pltpu.VMEM((WIN, part, size), F32)],
        3 * 6 * part * size**2, place, got, high, low,
    )

    def sent_to(flip):
        def target(y, c, zh, zl, x):
            return (y - 1) % sizes[0], c, zh ^ flip, zl, x
        return target

    back = [lax.ppermute(sent[flip], AXES, pairs_of(sizes, sent_to(flip))) for flip in range(2)]
    (result,) = call(order_kernel, 1, [(WIN, slots, piece, size)], [], 10**4, place, *back[::-1])
    return result[:, :, None]


def solution(mesh):
    sizes = (mesh.shape["row"] // 2, 2, 2, mesh.shape["col"] // 8, 4)
    fine = Mesh(mesh.devices.reshape(sizes), AXES)
    rows, cols = AXES[:2], AXES[2:]
    placed = (P(None, rows, None, cols, None, None), P(None, rows, None, cols, None, None), P())
    return jax.shard_map(
        lambda *args: on_device(sizes, *args),
        mesh=fine,
        in_specs=placed,
        out_specs=P(None, None, rows, cols, None),
        check_vma=False,
    )
```

```python
import functools
import math

import jax
import jax.numpy as jnp
import numpy as np
from jax import lax
from jax.experimental import pallas as pl
from jax.experimental.pallas import tpu as pltpu
from jax.sharding import Mesh, PartitionSpec as P

TOP = 4
WIN = 3
AXES = ("y", "core", "zh", "zl", "x")
F32 = jnp.float32


def pairs_of(sizes, target):
    pairs = []
    for number in range(math.prod(sizes)):
        there = target(*(int(i) for i in np.unravel_index(number, sizes)))
        if there is not None:
            pairs.append((number, int(np.ravel_multi_index(there, sizes))))
    return pairs


def halves(x):
    high = x.astype(jnp.bfloat16)
    return high, (x - high.astype(F32)).astype(jnp.bfloat16)


def times(a, b):
    dims = (((1,), (1,)), ((), ()))
    dot = functools.partial(lax.dot_general, dimension_numbers=dims, preferred_element_type=F32)
    return dot(a[0], b[0]) + (dot(a[0], b[1]) + dot(a[1], b[0]))


def codes_of(codes, tile):
    return codes[pl.ds(jnp.clip(tile, 0, codes.shape[0] - 1), 1), :]


def partners_of(code):
    return jnp.where(code == 0, 8, jnp.where(code == 1, 4, jnp.where(code == 2, 10, 5)))


def columns_of(codes, tiles):
    total = partners_of(codes_of(codes, tiles[0]))
    for k, tile in enumerate(tiles[1:], 1):
        total = total + (partners_of(codes_of(codes, tile)) << (4 * k))
    size = codes.shape[1]
    return jnp.broadcast_to(total, (size, size)).T


def columns_kernel(slots, place, codes, for_products, for_pack):
    row, half = place[0], place[2]
    rows_count = codes.shape[0] // slots
    for_products[...] = columns_of(codes, [slot * rows_count + row - 2 + e for e in (4, 3, 2) for slot in range(slots)])
    first = row + half * rows_count
    for_pack[...] = columns_of(codes, [first, first + 1])


def product_kernel(factor, place, left_ref, ahead_ref, beside_ref, codes, columns_ref, home_ref, sent, out, sems):
    row, col = place[0], place[1]
    slots, size = left_ref.shape[0], left_ref.shape[1]
    rows_count = codes.shape[0] // slots
    piece = size // codes.shape[0]
    chunks = size // out.shape[0] // piece
    col_bits = 1 << codes_of(codes, col)
    tile_rows = [slot * rows_count + row - 2 for slot in range(slots)]
    keys = [(slot, e) for e in (4, 3, 2) for slot in range(slots)]
    columns = columns_ref[...]
    gap = lax.broadcasted_iota(jnp.int32, (size, size), 1) - lax.broadcasted_iota(jnp.int32, (size, size), 0)
    lefts = [left_ref[jnp.where(row < 2, 0, slot)] for slot in range(slots)]
    left_halves = [halves(left) for left in lefts]
    copies = []
    for k, (slot, e) in enumerate(keys):
        tile_row = tile_rows[slot]
        other = slots - 1 - slot
        allowed = (columns & (col_bits << (4 * k))) != 0
        if e == 4:
            tile = ahead_ref[jnp.where(row >= rows_count - 2, other, slot)]
            allowed = allowed & (gap > 3 - (col - tile_row - e) * size)
        elif e == 3:
            tile = beside_ref[jnp.where(row >= rows_count - 1, other, slot)]
        else:
            tile = home_ref[slot]
        right = halves(jnp.where(allowed, tile, 0.0))
        live = (tile_row >= 0) & (col > tile_row + TOP)
        scale = jnp.where(live, factor, 0.0).astype(F32)
        own = jnp.where((tile_row >= 0) & (col == tile_row + e), 1.0, 0.0).astype(F32)
        full = scale * times(left_halves[slot], right) + own * lefts[slot]
        for x in range(out.shape[0]):
            for chunk in range(chunks):
                start = (chunk % slots) * (size // slots) + (chunk // slots * out.shape[0] + x) * piece
                out[x, TOP - e, slot, chunk * piece:(chunk + 1) * piece] = full[start:start + piece]
        copies.append(pltpu.make_async_copy(out.at[:, TOP - e, slot], sent.at[:, TOP - e, slot], sems.at[k]))
        copies[-1].start()
    for copy in copies:
        copy.wait()


def add_kernel(got, out):
    slots, rows = got.shape[2:4]
    deep = out.shape[0] // slots
    piece = rows // deep
    for number in range(WIN):
        for slot in range(slots):
            total = got[0, number, slot]
            for k in range(1, got.shape[0]):
                total = total + got[k, number, slot]
            for z in range(deep):
                out[slot * deep + z, number] = total[z * piece:(z + 1) * piece]


def pack_kernel(wide, place, codes, columns, gathered, next1, out):
    row, half, x = place[0], place[2], place[4]
    count, part, size = gathered.shape[0], gathered.shape[2], out.shape[3]
    first = row + half * (codes.shape[0] // 2)
    steps = lax.broadcasted_iota(jnp.int32, (part, size), 1) - lax.broadcasted_iota(jnp.int32, (part, size), 0)
    for i in range(count):
        start = pl.multiple_of((i * wide + x) * part, part)
        down = columns[pl.ds(start, part), :]
        for k, (at, beyond) in enumerate(((0, 1), (0, 2), (1, 1))):
            piece = gathered[i, k] if k < 2 else next1[i]
            allowed = (down & (1 << (codes_of(codes, first + at + beyond) + 4 * at))) != 0
            far = steps > 3 + start - beyond * size
            out[k, i] = jnp.where(allowed & far, piece, 0.0)


def assemble_kernel(order, place, *refs):
    packs, high, low, whole = refs[:-3], refs[-3], refs[-2], refs[-1]
    x = place[4]
    _, deep, part, _ = packs[0].shape
    for k in range(3):
        for j, pack in zip(order, packs):
            for i in range(deep):
                start = pl.multiple_of((i * len(packs) + (x ^ j)) * part, part)
                whole[k, pl.ds(start, part), :] = pack[k, i]
        high[k], low[k] = halves(whole[k])


def finish_kernel(factor, place, got, high, low, out_a, out_b, rows):
    half = place[2]
    sums = []
    for w in range(WIN):
        total = got[0, w]
        for k in range(1, got.shape[0]):
            total = total + got[k, w]
        sums.append(total)
    w4 = sums[0]
    w4_halves = halves(w4)
    w3 = sums[1] + factor * times(w4_halves, (high[2], low[2]))
    w2 = sums[2] + factor * (times(w4_halves, (high[1], low[1])) + times(halves(w3), (high[0], low[0])))
    piece = out_a.shape[1]
    for w, value in enumerate((w4, w3, w2)):
        rows[w] = value
        out_a[w] = rows[w, pl.ds(pl.multiple_of(half * piece, piece), piece), :]
        out_b[w] = rows[w, pl.ds(pl.multiple_of((1 - half) * piece, piece), piece), :]


def order_kernel(place, back1, back0, out):
    swap = (place[2] + place[6]) % 2 == 1
    out[:, 0] = jnp.where(swap, back1[...], back0[...])
    out[:, 1] = jnp.where(swap, back0[...], back1[...])


def call(kernel, in_count, outs, scratch, flops, *args, kind=F32, space=pltpu.VMEM):
    spec = pl.BlockSpec(memory_space=pltpu.VMEM)
    moved = sum(math.prod(a.shape) * 4 for a in args) + sum(math.prod(s) * 4 for s in outs)
    return pl.pallas_call(
        kernel,
        out_shape=[jax.ShapeDtypeStruct(s, kind) for s in outs],
        in_specs=[pl.BlockSpec(memory_space=pltpu.SMEM)] * in_count + [spec] * (len(args) - in_count),
        out_specs=[pl.BlockSpec(memory_space=space)] * len(outs),
        scratch_shapes=scratch,
        cost_estimate=pl.CostEstimate(flops=flops, bytes_accessed=moved, transcendentals=0),
        compiler_params=pltpu.CompilerParams(vmem_limit_bytes=24 * 1024 * 1024),
    )(*args)


def on_device(sizes, inside, outer, sequence):
    rows_count = sizes[0] * sizes[1]
    cols_count = sizes[2] * sizes[3] * sizes[4]
    size = inside.shape[-1]
    slots = inside.shape[0]
    tile_count = slots * rows_count
    part = slots * size // cols_count
    factor = 1.0 / math.sqrt(tile_count)
    core = lax.axis_index("core")
    row = lax.axis_index("y") * sizes[1] + core
    half = lax.axis_index("zh")
    col = lax.axis_index(AXES[2:])
    late = (row >= rows_count - 2).astype(jnp.int32)
    place = jnp.stack([row, col, half, core, lax.axis_index("x"), lax.axis_index("zl"), late]).astype(jnp.int32)
    home = inside[:, 0, 0, 0]
    out_tiles = outer[:, 0, 0, 0]

    def row_shift(v, by):
        n = sizes[0]
        return lax.ppermute(v, "y", [(i, (i + by) % n) for i in range(n)])

    left = row_shift(out_tiles, 1)
    beside = lax.ppermute(home, AXES[:2], [(i, (i - 1) % rows_count) for i in range(rows_count)])
    ahead = row_shift(home, -1)

    codes = sequence.reshape(tile_count, size)
    columns, pack_columns = call(
        functools.partial(columns_kernel, slots), 1, [(size, size)] * 2, [], 10**6, place, codes, kind=jnp.int32
    )

    spread = lax.all_to_all(home.reshape(cols_count, part, size), AXES[2:], 0, 0)
    spread, columns, pack_columns = lax.optimization_barrier((spread, columns, pack_columns))
    first = jnp.minimum(row + half * rows_count + 1, cols_count - 1)
    second = jnp.minimum(row + half * rows_count + 2, cols_count - 1)
    near1 = lax.dynamic_index_in_dim(spread, first, 0, False)
    near2 = lax.dynamic_index_in_dim(spread, second, 0, False)

    def previous_row(y, c, zh, zl, x):
        r = y * sizes[1] + c
        zh = zh if r > 0 else (zh + 1) % sizes[2]
        r = (r - 1) % rows_count
        return r // sizes[1], r % sizes[1], zh, zl, x

    near = jnp.stack([near1, near2])
    gathered = lax.all_to_all(jnp.broadcast_to(near, (sizes[3],) + near.shape), "zl", 0, 0)

    def partner(v, axis, n, j):
        return lax.ppermute(v, axis, [(i, i ^ j) for i in range(n)])

    wide = (sizes[4], WIN, slots, size // sizes[4], size)
    (parts,) = call(
        functools.partial(product_kernel, factor),
        1, [wide], [pltpu.VMEM(wide, F32), pltpu.SemaphoreType.DMA((WIN * slots,))], WIN * slots * 6 * size**3,
        place, left, ahead, beside, codes, columns, home, space=pl.ANY,
    )
    parts, gathered = lax.optimization_barrier((parts, gathered))
    next1 = lax.ppermute(gathered[:, 0], AXES, pairs_of(sizes, previous_row))
    (pack,) = call(
        functools.partial(pack_kernel, sizes[4]),
        1, [(3, sizes[3], part, size)], [], 10**6, place, codes, pack_columns, gathered, next1,
    )
    order = (0, 2, 3, 1)
    packs = [pack] + [partner(pack, "x", sizes[4], j) for j in order[1:]]
    high, low = call(
        functools.partial(assemble_kernel, order), 1, [(3, size, size)] * 2, [pltpu.VMEM((3, size, size), F32)], 2 * 10**10,
        place, *packs, kind=jnp.bfloat16,
    )
    parts = lax.all_to_all(parts, "x", 0, 0)
    parts, _ = lax.optimization_barrier((parts, pack))
    (ready,) = call(add_kernel, 0, [(slots * sizes[3], WIN, part, size)], [], 10**6, parts)
    got = lax.all_to_all(ready, ("zh", "zl"), 0, 0)
    piece = part // slots
    sent = call(
        functools.partial(finish_kernel, factor),
        1, [(WIN, piece, size)] * 2, [pltpu.VMEM((WIN, part, size), F32)],
        3 * 6 * part * size**2, place, got, high, low,
    )

    def sent_to(flip):
        def target(y, c, zh, zl, x):
            return (y - 1) % sizes[0], c, zh ^ flip, zl, x
        return target

    back = [lax.ppermute(sent[flip], AXES, pairs_of(sizes, sent_to(flip))) for flip in range(2)]
    (result,) = call(order_kernel, 1, [(WIN, slots, piece, size)], [], 10**4, place, *back[::-1])
    return result[:, :, None]


def solution(mesh):
    sizes = (mesh.shape["row"] // 2, 2, 2, mesh.shape["col"] // 8, 4)
    fine = Mesh(mesh.devices.reshape(sizes), AXES)
    rows, cols = AXES[:2], AXES[2:]
    placed = (P(None, rows, None, cols, None, None), P(None, rows, None, cols, None, None), P())
    return jax.shard_map(
        lambda *args: on_device(sizes, *args),
        mesh=fine,
        in_specs=placed,
        out_specs=P(None, None, rows, cols, None),
        check_vma=False,
    )
```

```python
import functools
import math

import jax
import jax.numpy as jnp
import numpy as np
from jax import lax
from jax.experimental import pallas as pl
from jax.experimental.pallas import tpu as pltpu
from jax.sharding import Mesh, PartitionSpec as P

TOP = 4
WIN = 3
AXES = ("y", "core", "zh", "zl", "x")
F32 = jnp.float32


def pairs_of(sizes, target):
    pairs = []
    for number in range(math.prod(sizes)):
        there = target(*(int(i) for i in np.unravel_index(number, sizes)))
        if there is not None:
            pairs.append((number, int(np.ravel_multi_index(there, sizes))))
    return pairs


def halves(x):
    high = x.astype(jnp.bfloat16)
    return high, (x - high.astype(F32)).astype(jnp.bfloat16)


def times(a, b):
    dims = (((1,), (1,)), ((), ()))
    dot = functools.partial(lax.dot_general, dimension_numbers=dims, preferred_element_type=F32)
    return dot(a[0], b[0]) + (dot(a[0], b[1]) + dot(a[1], b[0]))


def codes_of(codes, tile):
    return codes[pl.ds(jnp.clip(tile, 0, codes.shape[0] - 1), 1), :]


def partners_of(code):
    return jnp.where(code == 0, 8, jnp.where(code == 1, 4, jnp.where(code == 2, 10, 5)))


def columns_of(codes, tiles):
    total = partners_of(codes_of(codes, tiles[0]))
    for k, tile in enumerate(tiles[1:], 1):
        total = total + (partners_of(codes_of(codes, tile)) << (4 * k))
    size = codes.shape[1]
    return jnp.broadcast_to(total, (size, size)).T


def columns_kernel(slots, place, codes, for_products, for_pack):
    row, half = place[0], place[2]
    rows_count = codes.shape[0] // slots
    for_products[...] = columns_of(codes, [slot * rows_count + row - 2 + e for e in (4, 3, 2) for slot in range(slots)])
    first = row + half * rows_count
    for_pack[...] = columns_of(codes, [first, first + 1])


def product_kernel(factor, place, left_ref, ahead_ref, beside_ref, codes, columns_ref, home_ref, sent, out, sems):
    row, col = place[0], place[1]
    slots, size = left_ref.shape[0], left_ref.shape[1]
    rows_count = codes.shape[0] // slots
    piece = size // codes.shape[0]
    chunks = size // out.shape[0] // piece
    col_bits = 1 << codes_of(codes, col)
    tile_rows = [slot * rows_count + row - 2 for slot in range(slots)]
    keys = [(slot, e) for e in (4, 3, 2) for slot in range(slots)]
    columns = columns_ref[...]
    gap = lax.broadcasted_iota(jnp.int32, (size, size), 1) - lax.broadcasted_iota(jnp.int32, (size, size), 0)
    lefts = [left_ref[jnp.where(row < 2, 0, slot)] for slot in range(slots)]
    left_halves = [halves(left) for left in lefts]
    copies = []
    for k, (slot, e) in enumerate(keys):
        tile_row = tile_rows[slot]
        other = slots - 1 - slot
        allowed = (columns & (col_bits << (4 * k))) != 0
        if e == 4:
            tile = ahead_ref[jnp.where(row >= rows_count - 2, other, slot)]
            allowed = allowed & (gap > 3 - (col - tile_row - e) * size)
        elif e == 3:
            tile = beside_ref[jnp.where(row >= rows_count - 1, other, slot)]
        else:
            tile = home_ref[slot]
        right = halves(jnp.where(allowed, tile, 0.0))
        live = (tile_row >= 0) & (col > tile_row + TOP)
        scale = jnp.where(live, factor, 0.0).astype(F32)
        own = jnp.where((tile_row >= 0) & (col == tile_row + e), 1.0, 0.0).astype(F32)
        full = scale * times(left_halves[slot], right) + own * lefts[slot]
        for x in range(out.shape[0]):
            for chunk in range(chunks):
                start = (chunk % slots) * (size // slots) + (chunk // slots * out.shape[0] + x) * piece
                out[x, TOP - e, slot, chunk * piece:(chunk + 1) * piece] = full[start:start + piece]
        copies.append(pltpu.make_async_copy(out.at[:, TOP - e, slot], sent.at[:, TOP - e, slot], sems.at[k]))
        copies[-1].start()
    for copy in copies:
        copy.wait()


def add_kernel(got, out):
    slots, rows = got.shape[2:4]
    deep = out.shape[0] // slots
    piece = rows // deep
    for number in range(WIN):
        for slot in range(slots):
            total = got[0, number, slot]
            for k in range(1, got.shape[0]):
                total = total + got[k, number, slot]
            for z in range(deep):
                out[slot * deep + z, number] = total[z * piece:(z + 1) * piece]


def pack_kernel(wide, place, codes, columns, gathered, next1, out):
    row, half, x = place[0], place[2], place[4]
    count, part, size = gathered.shape[0], gathered.shape[2], out.shape[3]
    first = row + half * (codes.shape[0] // 2)
    steps = lax.broadcasted_iota(jnp.int32, (part, size), 1) - lax.broadcasted_iota(jnp.int32, (part, size), 0)
    for i in range(count):
        start = pl.multiple_of((i * wide + x) * part, part)
        down = columns[pl.ds(start, part), :]
        for k, (at, beyond) in enumerate(((0, 1), (0, 2), (1, 1))):
            piece = gathered[i, k] if k < 2 else next1[i]
            allowed = (down & (1 << (codes_of(codes, first + at + beyond) + 4 * at))) != 0
            far = steps > 3 + start - beyond * size
            out[k, i] = jnp.where(allowed & far, piece, 0.0)


def assemble_kernel(order, place, *refs):
    packs, high, low, whole = refs[:-3], refs[-3], refs[-2], refs[-1]
    x = place[4]
    _, deep, part, _ = packs[0].shape
    for k in range(3):
        for j, pack in zip(order, packs):
            for i in range(deep):
                start = pl.multiple_of((i * len(packs) + (x ^ j)) * part, part)
                whole[k, pl.ds(start, part), :] = pack[k, i]
        high[k], low[k] = halves(whole[k])


def finish_kernel(factor, place, got, high, low, out_a, out_b, rows):
    half = place[2]
    sums = []
    for w in range(WIN):
        total = got[0, w]
        for k in range(1, got.shape[0]):
            total = total + got[k, w]
        sums.append(total)
    w4 = sums[0]
    w4_halves = halves(w4)
    w3 = sums[1] + factor * times(w4_halves, (high[2], low[2]))
    w2 = sums[2] + factor * (times(w4_halves, (high[1], low[1])) + times(halves(w3), (high[0], low[0])))
    piece = out_a.shape[1]
    for w, value in enumerate((w4, w3, w2)):
        rows[w] = value
        out_a[w] = rows[w, pl.ds(pl.multiple_of(half * piece, piece), piece), :]
        out_b[w] = rows[w, pl.ds(pl.multiple_of((1 - half) * piece, piece), piece), :]


def order_kernel(place, back1, back0, out):
    swap = (place[2] + place[6]) % 2 == 1
    out[:, 0] = jnp.where(swap, back1[...], back0[...])
    out[:, 1] = jnp.where(swap, back0[...], back1[...])


def call(kernel, in_count, outs, scratch, flops, *args, kind=F32, space=pltpu.VMEM):
    spec = pl.BlockSpec(memory_space=pltpu.VMEM)
    moved = sum(math.prod(a.shape) * 4 for a in args) + sum(math.prod(s) * 4 for s in outs)
    return pl.pallas_call(
        kernel,
        out_shape=[jax.ShapeDtypeStruct(s, kind) for s in outs],
        in_specs=[pl.BlockSpec(memory_space=pltpu.SMEM)] * in_count + [spec] * (len(args) - in_count),
        out_specs=[pl.BlockSpec(memory_space=space)] * len(outs),
        scratch_shapes=scratch,
        cost_estimate=pl.CostEstimate(flops=flops, bytes_accessed=moved, transcendentals=0),
        compiler_params=pltpu.CompilerParams(vmem_limit_bytes=24 * 1024 * 1024),
    )(*args)


def on_device(sizes, inside, outer, sequence):
    rows_count = sizes[0] * sizes[1]
    cols_count = sizes[2] * sizes[3] * sizes[4]
    size = inside.shape[-1]
    slots = inside.shape[0]
    tile_count = slots * rows_count
    part = slots * size // cols_count
    factor = 1.0 / math.sqrt(tile_count)
    core = lax.axis_index("core")
    row = lax.axis_index("y") * sizes[1] + core
    half = lax.axis_index("zh")
    col = lax.axis_index(AXES[2:])
    late = (row >= rows_count - 2).astype(jnp.int32)
    place = jnp.stack([row, col, half, core, lax.axis_index("x"), lax.axis_index("zl"), late]).astype(jnp.int32)
    home = inside[:, 0, 0, 0]
    out_tiles = outer[:, 0, 0, 0]

    def row_shift(v, by):
        n = sizes[0]
        return lax.ppermute(v, "y", [(i, (i + by) % n) for i in range(n)])

    left = row_shift(out_tiles, 1)
    beside = lax.ppermute(home, AXES[:2], [(i, (i - 1) % rows_count) for i in range(rows_count)])
    ahead = row_shift(home, -1)

    codes = sequence.reshape(tile_count, size)
    columns, pack_columns = call(
        functools.partial(columns_kernel, slots), 1, [(size, size)] * 2, [], 10**6, place, codes, kind=jnp.int32
    )

    spread = lax.all_to_all(home.reshape(cols_count, part, size), AXES[2:], 0, 0)
    spread, columns, pack_columns = lax.optimization_barrier((spread, columns, pack_columns))
    first = jnp.minimum(row + half * rows_count + 1, cols_count - 1)
    second = jnp.minimum(row + half * rows_count + 2, cols_count - 1)
    near1 = lax.dynamic_index_in_dim(spread, first, 0, False)
    near2 = lax.dynamic_index_in_dim(spread, second, 0, False)

    def previous_row(y, c, zh, zl, x):
        r = y * sizes[1] + c
        zh = zh if r > 0 else (zh + 1) % sizes[2]
        r = (r - 1) % rows_count
        return r // sizes[1], r % sizes[1], zh, zl, x

    near = jnp.stack([near1, near2])
    gathered = lax.all_to_all(jnp.broadcast_to(near, (sizes[3],) + near.shape), "zl", 0, 0)

    def partner(v, axis, n, j):
        return lax.ppermute(v, axis, [(i, i ^ j) for i in range(n)])

    ahead, beside, gathered = lax.optimization_barrier((ahead, beside, gathered))
    wide = (sizes[4], WIN, slots, size // sizes[4], size)
    (parts,) = call(
        functools.partial(product_kernel, factor),
        1, [wide], [pltpu.VMEM(wide, F32), pltpu.SemaphoreType.DMA((WIN * slots,))], WIN * slots * 6 * size**3,
        place, left, ahead, beside, codes, columns, home, space=pl.ANY,
    )
    parts, gathered = lax.optimization_barrier((parts, gathered))
    next1 = lax.ppermute(gathered[:, 0], AXES, pairs_of(sizes, previous_row))
    (pack,) = call(
        functools.partial(pack_kernel, sizes[4]),
        1, [(3, sizes[3], part, size)], [], 10**6, place, codes, pack_columns, gathered, next1,
    )
    order = (0, 2, 3, 1)
    packs = [pack] + [partner(pack, "x", sizes[4], j) for j in order[1:]]
    high, low = call(
        functools.partial(assemble_kernel, order), 1, [(3, size, size)] * 2, [pltpu.VMEM((3, size, size), F32)], 2 * 10**10,
        place, *packs, kind=jnp.bfloat16,
    )
    parts = lax.all_to_all(parts, "x", 0, 0)
    parts, _ = lax.optimization_barrier((parts, pack))
    (ready,) = call(add_kernel, 0, [(slots * sizes[3], WIN, part, size)], [], 10**6, parts)
    got = lax.all_to_all(ready, ("zh", "zl"), 0, 0)
    piece = part // slots
    sent = call(
        functools.partial(finish_kernel, factor),
        1, [(WIN, piece, size)] * 2, [pltpu.VMEM((WIN, part, size), F32)],
        3 * 6 * part * size**2, place, got, high, low,
    )

    def sent_to(flip):
        def target(y, c, zh, zl, x):
            return (y - 1) % sizes[0], c, zh ^ flip, zl, x
        return target

    back = [lax.ppermute(sent[flip], AXES, pairs_of(sizes, sent_to(flip))) for flip in range(2)]
    (result,) = call(order_kernel, 1, [(WIN, slots, piece, size)], [], 10**4, place, *back[::-1])
    return result[:, :, None]


def solution(mesh):
    sizes = (mesh.shape["row"] // 2, 2, 2, mesh.shape["col"] // 8, 4)
    fine = Mesh(mesh.devices.reshape(sizes), AXES)
    rows, cols = AXES[:2], AXES[2:]
    placed = (P(None, rows, None, cols, None, None), P(None, rows, None, cols, None, None), P())
    return jax.shard_map(
        lambda *args: on_device(sizes, *args),
        mesh=fine,
        in_specs=placed,
        out_specs=P(None, None, rows, cols, None),
        check_vma=False,
    )
```

```python
import functools
import math

import jax
import jax.numpy as jnp
import numpy as np
from jax import lax
from jax.experimental import pallas as pl
from jax.experimental.pallas import tpu as pltpu
from jax.sharding import Mesh, PartitionSpec as P

TOP = 4
WIN = 3
AXES = ("y", "core", "zh", "zl", "x")
F32 = jnp.float32


def pairs_of(sizes, target):
    pairs = []
    for number in range(math.prod(sizes)):
        there = target(*(int(i) for i in np.unravel_index(number, sizes)))
        if there is not None:
            pairs.append((number, int(np.ravel_multi_index(there, sizes))))
    return pairs


def halves(x):
    high = x.astype(jnp.bfloat16)
    return high, (x - high.astype(F32)).astype(jnp.bfloat16)


def times(a, b):
    dims = (((1,), (1,)), ((), ()))
    dot = functools.partial(lax.dot_general, dimension_numbers=dims, preferred_element_type=F32)
    return dot(a[0], b[0]) + (dot(a[0], b[1]) + dot(a[1], b[0]))


def codes_of(codes, tile):
    return codes[pl.ds(jnp.clip(tile, 0, codes.shape[0] - 1), 1), :]


def partners_of(code):
    return jnp.where(code == 0, 8, jnp.where(code == 1, 4, jnp.where(code == 2, 10, 5)))


def columns_of(codes, tiles):
    total = partners_of(codes_of(codes, tiles[0]))
    for k, tile in enumerate(tiles[1:], 1):
        total = total + (partners_of(codes_of(codes, tile)) << (4 * k))
    size = codes.shape[1]
    return jnp.broadcast_to(total, (size, size)).T


def columns_kernel(slots, place, codes, for_products, for_pack):
    row, half = place[0], place[2]
    rows_count = codes.shape[0] // slots
    for_products[...] = columns_of(codes, [slot * rows_count + row - 2 + e for e in (4, 3, 2) for slot in range(slots)])
    first = row + half * rows_count
    for_pack[...] = columns_of(codes, [first, first + 1])


def product_kernel(factor, place, left_ref, ahead_ref, beside_ref, codes, columns_ref, home_ref, sent, out, sems):
    row, col = place[0], place[1]
    slots, size = left_ref.shape[0], left_ref.shape[1]
    rows_count = codes.shape[0] // slots
    piece = size // codes.shape[0]
    chunks = size // out.shape[0] // piece
    col_bits = 1 << codes_of(codes, col)
    tile_rows = [slot * rows_count + row - 2 for slot in range(slots)]
    keys = [(slot, e) for e in (4, 3, 2) for slot in range(slots)]
    columns = columns_ref[...]
    gap = lax.broadcasted_iota(jnp.int32, (size, size), 1) - lax.broadcasted_iota(jnp.int32, (size, size), 0)
    lefts = [left_ref[jnp.where(row < 2, 0, slot)] for slot in range(slots)]
    left_halves = [halves(left) for left in lefts]
    copies = []
    for k, (slot, e) in enumerate(keys):
        tile_row = tile_rows[slot]
        other = slots - 1 - slot
        allowed = (columns & (col_bits << (4 * k))) != 0
        if e == 4:
            tile = ahead_ref[jnp.where(row >= rows_count - 2, other, slot)]
            allowed = allowed & (gap > 3 - (col - tile_row - e) * size)
        elif e == 3:
            tile = beside_ref[jnp.where(row >= rows_count - 1, other, slot)]
        else:
            tile = home_ref[slot]
        right = halves(jnp.where(allowed, tile, 0.0))
        live = (tile_row >= 0) & (col > tile_row + TOP)
        scale = jnp.where(live, factor, 0.0).astype(F32)
        own = jnp.where((tile_row >= 0) & (col == tile_row + e), 1.0, 0.0).astype(F32)
        full = scale * times(left_halves[slot], right) + own * lefts[slot]
        for x in range(out.shape[0]):
            for chunk in range(chunks):
                start = (chunk % slots) * (size // slots) + (chunk // slots * out.shape[0] + x) * piece
                out[x, TOP - e, slot, chunk * piece:(chunk + 1) * piece] = full[start:start + piece]
        copies.append(pltpu.make_async_copy(out.at[:, TOP - e, slot], sent.at[:, TOP - e, slot], sems.at[k]))
        copies[-1].start()
    for copy in copies:
        copy.wait()


def add_kernel(got, out):
    slots, rows = got.shape[2:4]
    deep = out.shape[0] // slots
    piece = rows // deep
    for number in range(WIN):
        for slot in range(slots):
            total = got[0, number, slot]
            for k in range(1, got.shape[0]):
                total = total + got[k, number, slot]
            for z in range(deep):
                out[slot * deep + z, number] = total[z * piece:(z + 1) * piece]


def pack_kernel(wide, place, codes, columns, gathered, next1, out):
    row, half, x = place[0], place[2], place[4]
    count, part, size = gathered.shape[0], gathered.shape[2], out.shape[3]
    first = row + half * (codes.shape[0] // 2)
    steps = lax.broadcasted_iota(jnp.int32, (part, size), 1) - lax.broadcasted_iota(jnp.int32, (part, size), 0)
    for i in range(count):
        start = pl.multiple_of((i * wide + x) * part, part)
        down = columns[pl.ds(start, part), :]
        for k, (at, beyond) in enumerate(((0, 1), (0, 2), (1, 1))):
            piece = gathered[i, k] if k < 2 else next1[i]
            allowed = (down & (1 << (codes_of(codes, first + at + beyond) + 4 * at))) != 0
            far = steps > 3 + start - beyond * size
            out[k, i] = jnp.where(allowed & far, piece, 0.0)


def assemble_kernel(order, place, *refs):
    packs, high, low, whole = refs[:-3], refs[-3], refs[-2], refs[-1]
    x = place[4]
    _, deep, part, _ = packs[0].shape
    for k in range(3):
        for j, pack in zip(order, packs):
            for i in range(deep):
                start = pl.multiple_of((i * len(packs) + (x ^ j)) * part, part)
                whole[k, pl.ds(start, part), :] = pack[k, i]
        high[k], low[k] = halves(whole[k])


def finish_kernel(factor, place, got, high, low, out_a, out_b, rows):
    half = place[2]
    sums = []
    for w in range(WIN):
        total = got[0, w]
        for k in range(1, got.shape[0]):
            total = total + got[k, w]
        sums.append(total)
    w4 = sums[0]
    w4_halves = halves(w4)
    w3 = sums[1] + factor * times(w4_halves, (high[2], low[2]))
    w2 = sums[2] + factor * (times(w4_halves, (high[1], low[1])) + times(halves(w3), (high[0], low[0])))
    piece = out_a.shape[1]
    for w, value in enumerate((w4, w3, w2)):
        rows[w] = value
        out_a[w] = rows[w, pl.ds(pl.multiple_of(half * piece, piece), piece), :]
        out_b[w] = rows[w, pl.ds(pl.multiple_of((1 - half) * piece, piece), piece), :]


def order_kernel(place, back1, back0, out):
    swap = (place[2] + place[6]) % 2 == 1
    out[:, 0] = jnp.where(swap, back1[...], back0[...])
    out[:, 1] = jnp.where(swap, back0[...], back1[...])


def call(kernel, in_count, outs, scratch, flops, *args, kind=F32, space=pltpu.VMEM):
    spec = pl.BlockSpec(memory_space=pltpu.VMEM)
    moved = sum(math.prod(a.shape) * 4 for a in args) + sum(math.prod(s) * 4 for s in outs)
    return pl.pallas_call(
        kernel,
        out_shape=[jax.ShapeDtypeStruct(s, kind) for s in outs],
        in_specs=[pl.BlockSpec(memory_space=pltpu.SMEM)] * in_count + [spec] * (len(args) - in_count),
        out_specs=[pl.BlockSpec(memory_space=space)] * len(outs),
        scratch_shapes=scratch,
        cost_estimate=pl.CostEstimate(flops=flops, bytes_accessed=moved, transcendentals=0),
        compiler_params=pltpu.CompilerParams(vmem_limit_bytes=24 * 1024 * 1024),
    )(*args)


def on_device(sizes, inside, outer, sequence):
    rows_count = sizes[0] * sizes[1]
    cols_count = sizes[2] * sizes[3] * sizes[4]
    size = inside.shape[-1]
    slots = inside.shape[0]
    tile_count = slots * rows_count
    part = slots * size // cols_count
    factor = 1.0 / math.sqrt(tile_count)
    core = lax.axis_index("core")
    row = lax.axis_index("y") * sizes[1] + core
    half = lax.axis_index("zh")
    col = lax.axis_index(AXES[2:])
    late = (row >= rows_count - 2).astype(jnp.int32)
    place = jnp.stack([row, col, half, core, lax.axis_index("x"), lax.axis_index("zl"), late]).astype(jnp.int32)
    home = inside[:, 0, 0, 0]
    out_tiles = outer[:, 0, 0, 0]

    def row_shift(v, by):
        n = sizes[0]
        return lax.ppermute(v, "y", [(i, (i + by) % n) for i in range(n)])

    left = row_shift(out_tiles, 1)
    beside = lax.ppermute(home, AXES[:2], [(i, (i - 1) % rows_count) for i in range(rows_count)])
    ahead = row_shift(home, -1)

    codes = sequence.reshape(tile_count, size)
    columns, pack_columns = call(
        functools.partial(columns_kernel, slots), 1, [(size, size)] * 2, [], 10**6, place, codes, kind=jnp.int32
    )

    spread = lax.all_to_all(home.reshape(cols_count, part, size), AXES[2:], 0, 0)
    spread, columns, pack_columns = lax.optimization_barrier((spread, columns, pack_columns))
    first = jnp.minimum(row + half * rows_count + 1, cols_count - 1)
    second = jnp.minimum(row + half * rows_count + 2, cols_count - 1)
    near1 = lax.dynamic_index_in_dim(spread, first, 0, False)
    near2 = lax.dynamic_index_in_dim(spread, second, 0, False)

    def previous_row(y, c, zh, zl, x):
        r = y * sizes[1] + c
        zh = zh if r > 0 else (zh + 1) % sizes[2]
        r = (r - 1) % rows_count
        return r // sizes[1], r % sizes[1], zh, zl, x

    near = jnp.stack([near1, near2])
    gathered = lax.all_to_all(jnp.broadcast_to(near, (sizes[3],) + near.shape), "zl", 0, 0)

    def partner(v, axis, n, j):
        return lax.ppermute(v, axis, [(i, i ^ j) for i in range(n)])

    ahead, beside, gathered = lax.optimization_barrier((ahead, beside, gathered))
    wide = (sizes[4], WIN, slots, size // sizes[4], size)
    (parts,) = call(
        functools.partial(product_kernel, factor),
        1, [wide], [pltpu.VMEM(wide, F32), pltpu.SemaphoreType.DMA((WIN * slots,))], WIN * slots * 6 * size**3,
        place, left, ahead, beside, codes, columns, home, space=pl.ANY,
    )
    parts, gathered = lax.optimization_barrier((parts, gathered))
    next1 = lax.ppermute(gathered[:, 0], AXES, pairs_of(sizes, previous_row))
    (pack,) = call(
        functools.partial(pack_kernel, sizes[4]),
        1, [(3, sizes[3], part, size)], [], 10**6, place, codes, pack_columns, gathered, next1,
    )
    parts = lax.all_to_all(parts, "x", 0, 0)
    parts, later = lax.optimization_barrier((parts, pack))
    order = (0, 2, 3, 1)
    packs = [pack] + [partner(later if j == 2 else pack, "x", sizes[4], j) for j in order[1:]]
    high, low = call(
        functools.partial(assemble_kernel, order), 1, [(3, size, size)] * 2, [pltpu.VMEM((3, size, size), F32)], 2 * 10**10,
        place, *packs, kind=jnp.bfloat16,
    )
    (ready,) = call(add_kernel, 0, [(slots * sizes[3], WIN, part, size)], [], 10**6, parts)
    got = lax.all_to_all(ready, ("zh", "zl"), 0, 0)
    piece = part // slots
    sent = call(
        functools.partial(finish_kernel, factor),
        1, [(WIN, piece, size)] * 2, [pltpu.VMEM((WIN, part, size), F32)],
        3 * 6 * part * size**2, place, got, high, low,
    )

    def sent_to(flip):
        def target(y, c, zh, zl, x):
            return (y - 1) % sizes[0], c, zh ^ flip, zl, x
        return target

    back = [lax.ppermute(sent[flip], AXES, pairs_of(sizes, sent_to(flip))) for flip in range(2)]
    (result,) = call(order_kernel, 1, [(WIN, slots, piece, size)], [], 10**4, place, *back[::-1])
    return result[:, :, None]


def solution(mesh):
    sizes = (mesh.shape["row"] // 2, 2, 2, mesh.shape["col"] // 8, 4)
    fine = Mesh(mesh.devices.reshape(sizes), AXES)
    rows, cols = AXES[:2], AXES[2:]
    placed = (P(None, rows, None, cols, None, None), P(None, rows, None, cols, None, None), P())
    return jax.shard_map(
        lambda *args: on_device(sizes, *args),
        mesh=fine,
        in_specs=placed,
        out_specs=P(None, None, rows, cols, None),
        check_vma=False,
    )
```

```python
import functools
import math

import jax
import jax.numpy as jnp
import numpy as np
from jax import lax
from jax.experimental import pallas as pl
from jax.experimental.pallas import tpu as pltpu
from jax.sharding import Mesh, PartitionSpec as P

TOP = 4
WIN = 3
AXES = ("y", "core", "zh", "zl", "x")
F32 = jnp.float32


def pairs_of(sizes, target):
    pairs = []
    for number in range(math.prod(sizes)):
        there = target(*(int(i) for i in np.unravel_index(number, sizes)))
        if there is not None:
            pairs.append((number, int(np.ravel_multi_index(there, sizes))))
    return pairs


def halves(x):
    high = x.astype(jnp.bfloat16)
    return high, (x - high.astype(F32)).astype(jnp.bfloat16)


def times(a, b):
    dims = (((1,), (1,)), ((), ()))
    dot = functools.partial(lax.dot_general, dimension_numbers=dims, preferred_element_type=F32)
    rows = a[0].shape[0]
    both = dot(jnp.concatenate([a[0], a[1]], axis=0), b[0])
    return both[:rows] + (dot(a[0], b[1]) + both[rows:])


def codes_of(codes, tile):
    return codes[pl.ds(jnp.clip(tile, 0, codes.shape[0] - 1), 1), :]


def partners_of(code):
    return jnp.where(code == 0, 8, jnp.where(code == 1, 4, jnp.where(code == 2, 10, 5)))


def columns_of(codes, tiles):
    total = partners_of(codes_of(codes, tiles[0]))
    for k, tile in enumerate(tiles[1:], 1):
        total = total + (partners_of(codes_of(codes, tile)) << (4 * k))
    size = codes.shape[1]
    return jnp.broadcast_to(total, (size, size)).T


def columns_kernel(slots, place, codes, for_products, for_pack):
    row, half = place[0], place[2]
    rows_count = codes.shape[0] // slots
    for_products[...] = columns_of(codes, [slot * rows_count + row - 2 + e for e in (4, 3, 2) for slot in range(slots)])
    first = row + half * rows_count
    for_pack[...] = columns_of(codes, [first, first + 1])


def product_kernel(factor, place, left_ref, ahead_ref, beside_ref, codes, columns_ref, home_ref, sent, out, sems):
    row, col = place[0], place[1]
    slots, size = left_ref.shape[0], left_ref.shape[1]
    rows_count = codes.shape[0] // slots
    piece = size // codes.shape[0]
    chunks = size // out.shape[0] // piece
    col_bits = 1 << codes_of(codes, col)
    tile_rows = [slot * rows_count + row - 2 for slot in range(slots)]
    keys = [(slot, e) for e in (4, 3, 2) for slot in range(slots)]
    columns = columns_ref[...]
    gap = lax.broadcasted_iota(jnp.int32, (size, size), 1) - lax.broadcasted_iota(jnp.int32, (size, size), 0)
    lefts = [left_ref[jnp.where(row < 2, 0, slot)] for slot in range(slots)]
    left_halves = [halves(left) for left in lefts]
    copies = []
    for k, (slot, e) in enumerate(keys):
        tile_row = tile_rows[slot]
        other = slots - 1 - slot
        allowed = (columns & (col_bits << (4 * k))) != 0
        if e == 4:
            tile = ahead_ref[jnp.where(row >= rows_count - 2, other, slot)]
            allowed = allowed & (gap > 3 - (col - tile_row - e) * size)
        elif e == 3:
            tile = beside_ref[jnp.where(row >= rows_count - 1, other, slot)]
        else:
            tile = home_ref[slot]
        right = halves(jnp.where(allowed, tile, 0.0))
        live = (tile_row >= 0) & (col > tile_row + TOP)
        scale = jnp.where(live, factor, 0.0).astype(F32)
        own = jnp.where((tile_row >= 0) & (col == tile_row + e), 1.0, 0.0).astype(F32)
        full = scale * times(left_halves[slot], right) + own * lefts[slot]
        for x in range(out.shape[0]):
            for chunk in range(chunks):
                start = (chunk % slots) * (size // slots) + (chunk // slots * out.shape[0] + x) * piece
                out[x, TOP - e, slot, chunk * piece:(chunk + 1) * piece] = full[start:start + piece]
        copies.append(pltpu.make_async_copy(out.at[:, TOP - e, slot], sent.at[:, TOP - e, slot], sems.at[k]))
        copies[-1].start()
    for copy in copies:
        copy.wait()


def add_kernel(got, out):
    slots, rows = got.shape[2:4]
    deep = out.shape[0] // slots
    piece = rows // deep
    for number in range(WIN):
        for slot in range(slots):
            total = got[0, number, slot]
            for k in range(1, got.shape[0]):
                total = total + got[k, number, slot]
            for z in range(deep):
                out[slot * deep + z, number] = total[z * piece:(z + 1) * piece]


def pack_kernel(wide, place, codes, columns, gathered, next1, out):
    row, half, x = place[0], place[2], place[4]
    count, part, size = gathered.shape[0], gathered.shape[2], out.shape[3]
    first = row + half * (codes.shape[0] // 2)
    steps = lax.broadcasted_iota(jnp.int32, (part, size), 1) - lax.broadcasted_iota(jnp.int32, (part, size), 0)
    for i in range(count):
        start = pl.multiple_of((i * wide + x) * part, part)
        down = columns[pl.ds(start, part), :]
        for k, (at, beyond) in enumerate(((0, 1), (0, 2), (1, 1))):
            piece = gathered[i, k] if k < 2 else next1[i]
            allowed = (down & (1 << (codes_of(codes, first + at + beyond) + 4 * at))) != 0
            far = steps > 3 + start - beyond * size
            out[k, i] = jnp.where(allowed & far, piece, 0.0)


def assemble_kernel(order, place, *refs):
    packs, high, low, whole = refs[:-3], refs[-3], refs[-2], refs[-1]
    x = place[4]
    _, deep, part, _ = packs[0].shape
    for k in range(3):
        for j, pack in zip(order, packs):
            for i in range(deep):
                start = pl.multiple_of((i * len(packs) + (x ^ j)) * part, part)
                whole[k, pl.ds(start, part), :] = pack[k, i]
        high[k], low[k] = halves(whole[k])


def finish_kernel(factor, place, got, high, low, out_a, out_b, rows):
    half = place[2]
    sums = []
    for w in range(WIN):
        total = got[0, w]
        for k in range(1, got.shape[0]):
            total = total + got[k, w]
        sums.append(total)
    w4 = sums[0]
    w4_halves = halves(w4)
    w3 = sums[1] + factor * times(w4_halves, (high[2], low[2]))
    w2 = sums[2] + factor * (times(w4_halves, (high[1], low[1])) + times(halves(w3), (high[0], low[0])))
    piece = out_a.shape[1]
    for w, value in enumerate((w4, w3, w2)):
        rows[w] = value
        out_a[w] = rows[w, pl.ds(pl.multiple_of(half * piece, piece), piece), :]
        out_b[w] = rows[w, pl.ds(pl.multiple_of((1 - half) * piece, piece), piece), :]


def order_kernel(place, back1, back0, out):
    swap = (place[2] + place[6]) % 2 == 1
    out[:, 0] = jnp.where(swap, back1[...], back0[...])
    out[:, 1] = jnp.where(swap, back0[...], back1[...])


def call(kernel, in_count, outs, scratch, flops, *args, kind=F32, space=pltpu.VMEM):
    spec = pl.BlockSpec(memory_space=pltpu.VMEM)
    moved = sum(math.prod(a.shape) * 4 for a in args) + sum(math.prod(s) * 4 for s in outs)
    return pl.pallas_call(
        kernel,
        out_shape=[jax.ShapeDtypeStruct(s, kind) for s in outs],
        in_specs=[pl.BlockSpec(memory_space=pltpu.SMEM)] * in_count + [spec] * (len(args) - in_count),
        out_specs=[pl.BlockSpec(memory_space=space)] * len(outs),
        scratch_shapes=scratch,
        cost_estimate=pl.CostEstimate(flops=flops, bytes_accessed=moved, transcendentals=0),
        compiler_params=pltpu.CompilerParams(vmem_limit_bytes=24 * 1024 * 1024),
    )(*args)


def on_device(sizes, inside, outer, sequence):
    rows_count = sizes[0] * sizes[1]
    cols_count = sizes[2] * sizes[3] * sizes[4]
    size = inside.shape[-1]
    slots = inside.shape[0]
    tile_count = slots * rows_count
    part = slots * size // cols_count
    factor = 1.0 / math.sqrt(tile_count)
    core = lax.axis_index("core")
    row = lax.axis_index("y") * sizes[1] + core
    half = lax.axis_index("zh")
    col = lax.axis_index(AXES[2:])
    late = (row >= rows_count - 2).astype(jnp.int32)
    place = jnp.stack([row, col, half, core, lax.axis_index("x"), lax.axis_index("zl"), late]).astype(jnp.int32)
    home = inside[:, 0, 0, 0]
    out_tiles = outer[:, 0, 0, 0]

    def row_shift(v, by):
        n = sizes[0]
        return lax.ppermute(v, "y", [(i, (i + by) % n) for i in range(n)])

    left = row_shift(out_tiles, 1)
    beside = lax.ppermute(home, AXES[:2], [(i, (i - 1) % rows_count) for i in range(rows_count)])
    ahead = row_shift(home, -1)

    codes = sequence.reshape(tile_count, size)
    columns, pack_columns = call(
        functools.partial(columns_kernel, slots), 1, [(size, size)] * 2, [], 10**6, place, codes, kind=jnp.int32
    )

    spread = lax.all_to_all(home.reshape(cols_count, part, size), AXES[2:], 0, 0)
    spread, columns, pack_columns = lax.optimization_barrier((spread, columns, pack_columns))
    first = jnp.minimum(row + half * rows_count + 1, cols_count - 1)
    second = jnp.minimum(row + half * rows_count + 2, cols_count - 1)
    near1 = lax.dynamic_index_in_dim(spread, first, 0, False)
    near2 = lax.dynamic_index_in_dim(spread, second, 0, False)

    def previous_row(y, c, zh, zl, x):
        r = y * sizes[1] + c
        zh = zh if r > 0 else (zh + 1) % sizes[2]
        r = (r - 1) % rows_count
        return r // sizes[1], r % sizes[1], zh, zl, x

    near = jnp.stack([near1, near2])
    gathered = lax.all_to_all(jnp.broadcast_to(near, (sizes[3],) + near.shape), "zl", 0, 0)

    def partner(v, axis, n, j):
        return lax.ppermute(v, axis, [(i, i ^ j) for i in range(n)])

    ahead, beside, gathered = lax.optimization_barrier((ahead, beside, gathered))
    wide = (sizes[4], WIN, slots, size // sizes[4], size)
    (parts,) = call(
        functools.partial(product_kernel, factor),
        1, [wide], [pltpu.VMEM(wide, F32), pltpu.SemaphoreType.DMA((WIN * slots,))], WIN * slots * 6 * size**3,
        place, left, ahead, beside, codes, columns, home, space=pl.ANY,
    )
    parts, gathered = lax.optimization_barrier((parts, gathered))
    next1 = lax.ppermute(gathered[:, 0], AXES, pairs_of(sizes, previous_row))
    (pack,) = call(
        functools.partial(pack_kernel, sizes[4]),
        1, [(3, sizes[3], part, size)], [], 10**6, place, codes, pack_columns, gathered, next1,
    )
    order = (0, 2, 3, 1)
    packs = [pack] + [partner(pack, "x", sizes[4], j) for j in order[1:]]
    high, low = call(
        functools.partial(assemble_kernel, order), 1, [(3, size, size)] * 2, [pltpu.VMEM((3, size, size), F32)], 2 * 10**10,
        place, *packs, kind=jnp.bfloat16,
    )
    parts = lax.all_to_all(parts, "x", 0, 0)
    parts, _ = lax.optimization_barrier((parts, pack))
    (ready,) = call(add_kernel, 0, [(slots * sizes[3], WIN, part, size)], [], 10**6, parts)
    got = lax.all_to_all(ready, ("zh", "zl"), 0, 0)
    piece = part // slots
    sent = call(
        functools.partial(finish_kernel, factor),
        1, [(WIN, piece, size)] * 2, [pltpu.VMEM((WIN, part, size), F32)],
        3 * 6 * part * size**2, place, got, high, low,
    )

    def sent_to(flip):
        def target(y, c, zh, zl, x):
            return (y - 1) % sizes[0], c, zh ^ flip, zl, x
        return target

    back = [lax.ppermute(sent[flip], AXES, pairs_of(sizes, sent_to(flip))) for flip in range(2)]
    (result,) = call(order_kernel, 1, [(WIN, slots, piece, size)], [], 10**4, place, *back[::-1])
    return result[:, :, None]


def solution(mesh):
    sizes = (mesh.shape["row"] // 2, 2, 2, mesh.shape["col"] // 8, 4)
    fine = Mesh(mesh.devices.reshape(sizes), AXES)
    rows, cols = AXES[:2], AXES[2:]
    placed = (P(None, rows, None, cols, None, None), P(None, rows, None, cols, None, None), P())
    return jax.shard_map(
        lambda *args: on_device(sizes, *args),
        mesh=fine,
        in_specs=placed,
        out_specs=P(None, None, rows, cols, None),
        check_vma=False,
    )
```
